32 devices in a mesh: dp: 2 (over core), seq: 16 (over z, y, x).
Axes of the slice: x: 2, y: 2, z: 4, core: 2. Of those that a mesh axis runs over, the one named last changes fastest.
Arguments:
- block_input: bfloat16 [2, 2048, 2048], P('dp', 'seq'), may hold values from -6 to 6
- segments: int32 [2, 2048], P('dp', 'seq'), may hold values from 0 to 3, as said below
- mix_gain: float32 [2048], P(('dp', 'seq')), may hold values from 0.5 to 1.5
- w_project: float32 [2048, 6144], P(('dp', 'seq')), may hold values from -0.125 to 0.125
- conv_taps: float32 [4, 6144], P(None, ('dp', 'seq')), may hold values from -3 to 3
- w_beta: float32 [2048, 16], P(('dp', 'seq')), may hold values from -0.125 to 0.125
- w_gate: float32 [2048, 2048], P(('dp', 'seq')), may hold values from -0.125 to 0.125
- head_gain: float32 [2048], P(('dp', 'seq')), may hold values from 0.5 to 1.5
- w_output: float32 [2048, 2048], P(('dp', 'seq')), may hold values from -0.1875 to 0.1875
- ffn_gain: float32 [2048], P(('dp', 'seq')), may hold values from 0.5 to 1.5
- w_hidden_gate: float32 [2048, 5632], P(('dp', 'seq')), may hold values from -0.125 to 0.125
- w_hidden_up: float32 [2048, 5632], P(('dp', 'seq')), may hold values from -0.125 to 0.125
- w_hidden_down: float32 [5632, 2048], P(('dp', 'seq')), may hold values from -0.109375 to 0.109375
- cotangent: bfloat16 [2, 2048, 2048], P('dp', 'seq'), may hold values from -6 to 6
Outputs:
- block_output: bfloat16 [2, 2048, 2048], P('dp', 'seq')
- grad_input: float32 [2, 2048, 2048], P('dp', 'seq')
- grad_mix_gain: float32 [2048], P(('dp', 'seq'))
- grad_project: float32 [2048, 6144], P(('dp', 'seq'))
- grad_conv_taps: float32 [4, 6144], P(None, ('dp', 'seq'))
- grad_beta: float32 [2048, 16], P(('dp', 'seq'))
- grad_gate: float32 [2048, 2048], P(('dp', 'seq'))
- grad_head_gain: float32 [2048], P(('dp', 'seq'))
- grad_output: float32 [2048, 2048], P(('dp', 'seq'))
- grad_ffn_gain: float32 [2048], P(('dp', 'seq'))
- grad_hidden_gate: float32 [2048, 5632], P(('dp', 'seq'))
- grad_hidden_up: float32 [2048, 5632], P(('dp', 'seq'))
- grad_hidden_down: float32 [5632, 2048], P(('dp', 'seq'))
The draws below stay inside these ranges and needn't reach their ends.
Inputs may be any that keep to these rules, and one draw needn't show every extreme that they name: In every row the ids never fall; segment 1 begins within the first 128 slots and ends within the last 128 slots; segments 0, 2 and 3 each hold at least one slot.
All inputs are finite; a program needn't handle non-finite values.
Results may differ from the reference program's by a relative error of at most 0.015.
The reference program's roundings to bfloat16 on the way (of `normed`, `projected`, `scaled`, `normed_two` and `hidden`) count: a program that leaves them out, or rounds other values in their place, can miss the bound.
Values may be sent and summed in bfloat16 or wider, within the bound.
No kernel may reach another device: no remote copies, remote signals or barrier semaphores. Data moves between devices by JAX's collectives and lax.ppermute only.
A program may use at most 512 MiB of HBM per device.

```python
import jax
import jax.numpy as jnp
from jax import lax

D = 2048
H = 16
HEAD = 128
FF = 5632
CONV = 4
GROUP = 64
TOK_DEV = 128
ROW_LEN = 2048
ROWS = 2


def draw_segments(key, part):
    key = jax.random.fold_in(key, 7)
    keys = jax.random.split(key, 3)
    first_end = jax.random.randint(keys[0], (ROWS, 1), 1, TOK_DEV)
    tail = jax.random.randint(keys[1], (ROWS, 1), 2, TOK_DEV)
    third = jax.random.randint(keys[2], (ROWS, 1), 1, tail)
    second_end = ROW_LEN - tail
    third_end = second_end + third
    position = jnp.arange(ROW_LEN, dtype=jnp.int32)[None, :]
    ids = (position >= first_end).astype(jnp.int32) + (position >= second_end).astype(jnp.int32) + (position >= third_end).astype(jnp.int32)
    return ids.astype(jnp.int32)


def block_scale(key, shape, shards, low, top_value):
    loudness, own = 1.0, jax.random.fold_in(key, 6)
    for axis_at, blocks in shards:
        steps = jnp.exp(jax.random.uniform(jax.random.fold_in(own, axis_at), (blocks,), jnp.float32, low / len(shards), top_value / len(shards)))
        loudness = loudness * jnp.repeat(steps, shape[axis_at] // blocks).reshape([-1 if axis == axis_at else 1 for axis in range(len(shape))])
    return loudness


def scatter_about(own_key, extent, deviation, reach, shards=(), kind=jnp.bfloat16):
    values = jax.random.normal(own_key, extent, jnp.float32) * deviation
    if len(shards) > 0:
        values = block_scale(own_key, extent, shards, -0.22, 0.18) * values
    return jnp.clip(values, min=-reach, max=reach).astype(kind)


def setup_inputs(seed: int = 0) -> dict:
    seeds = jax.random.split(jax.random.key(seed), 15)
    block_input = scatter_about(seeds[0], (ROWS, ROW_LEN, D), 1.0, 6.0, ((0, 2), (1, 16)))
    segments = draw_segments(jax.random.fold_in(seeds[14], 71), 0)
    mix_gain = jnp.clip(1.0 + 0.1 * jax.random.normal(seeds[2], (D,), jnp.float32), 0.5, 1.5)
    w_project = scatter_about(seeds[3], (D, 3 * D), D ** -0.5, 0.125, ((0, 32),), jnp.float32)
    conv_taps = scatter_about(seeds[4], (CONV, 3 * D), 0.5, 3.0, ((1, 32),), jnp.float32)
    w_beta = scatter_about(seeds[5], (D, H), D ** -0.5, 0.125, ((0, 32),), jnp.float32)
    w_gate = scatter_about(seeds[6], (D, D), D ** -0.5, 0.125, ((0, 32),), jnp.float32)
    head_gain = jnp.clip(1.0 + 0.1 * jax.random.normal(seeds[7], (D,), jnp.float32), 0.5, 1.5)
    w_output = scatter_about(seeds[8], (D, D), (D // 2) ** -0.5, 0.1875, ((0, 32),), jnp.float32)
    ffn_gain = jnp.clip(1.0 + 0.1 * jax.random.normal(seeds[9], (D,), jnp.float32), 0.5, 1.5)
    w_hidden_gate = scatter_about(seeds[10], (D, FF), D ** -0.5, 0.125, ((0, 32),), jnp.float32)
    w_hidden_up = scatter_about(seeds[11], (D, FF), D ** -0.5, 0.125, ((0, 32),), jnp.float32)
    w_hidden_down = scatter_about(seeds[12], (FF, D), (FF // 2) ** -0.5, 0.109375, ((0, 32),), jnp.float32)
    cotangent = scatter_about(seeds[13], (ROWS, ROW_LEN, D), 1.0, 6.0, ((0, 2), (1, 16)))
    return dict(block_input=block_input, segments=segments, mix_gain=mix_gain, w_project=w_project, conv_taps=conv_taps, w_beta=w_beta, w_gate=w_gate, head_gain=head_gain, w_output=w_output, ffn_gain=ffn_gain, w_hidden_gate=w_hidden_gate, w_hidden_up=w_hidden_up, w_hidden_down=w_hidden_down, cotangent=cotangent)


EPS = 1e-06
HEAD_EPS = 0.01
HIGH = lax.Precision.HIGHEST

@jax.custom_vjp
def low(v):
    return lax.optimization_barrier(v.astype(jnp.bfloat16)).astype(jnp.float32)

@jax.custom_vjp
def low_back(v):
    return v

def low_keep(v):
    return (low(v), None)

def low_pass(kept, grad):
    return (grad,)

def back_keep(v):
    return (v, None)

def back_low(kept, grad):
    return (low(grad),)
low.defvjp(low_keep, low_pass)
low_back.defvjp(back_keep, back_low)

def rms_scale(values, gain):
    return values * lax.rsqrt(lax.optimization_barrier(jnp.mean(values * values, axis=-1, keepdims=True)) + EPS) * gain

def head_scale(values, gain):
    return values * lax.rsqrt(lax.optimization_barrier(jnp.mean(values * values, axis=-1, keepdims=True)) + HEAD_EPS) * gain

def unit_rows(values):
    return values * lax.rsqrt(lax.optimization_barrier(jnp.sum(values * values, axis=-1, keepdims=True)) + EPS)

def matmul(left, right):
    return jnp.dot(left, right, precision=HIGH)

def short_conv(projected, segment, taps):
    padded = jnp.concatenate([jnp.zeros((CONV - 1, projected.shape[1]), jnp.float32), projected], 0)
    seg_padded = jnp.concatenate([jnp.full((CONV - 1,), -1, jnp.int32), segment.astype(jnp.int32)], 0)
    total = jnp.zeros_like(projected)
    for tap in range(CONV):
        same = (seg_padded[tap:tap + ROW_LEN] == segment).astype(jnp.float32)
        total = total + taps[tap] * padded[tap:tap + ROW_LEN] * same[:, None]
    return total

def token_step(state, item):
    query, key, value, strength, start = item
    state = state * (1.0 - start)
    recall = jnp.einsum('hvk,hk->hv', state, key, precision=HIGH)
    state = state + strength[:, None, None] * jnp.einsum('hv,hk->hvk', value - recall, key, precision=HIGH)
    output = jnp.einsum('hvk,hk->hv', state, query, precision=HIGH)
    return (state, output)

def block_run(state, items):
    return lax.scan(token_step, state, items)

def delta_row(query, key, value, strength, start):
    blocks = ROW_LEN // GROUP
    items = tuple((a.reshape((blocks, GROUP) + a.shape[1:]) for a in (query, key, value, strength, start)))
    state = jnp.zeros((H, HEAD, HEAD), jnp.float32)
    state, outputs = lax.scan(jax.checkpoint(block_run), state, items)
    return outputs.reshape(ROW_LEN, H, HEAD)

def layer(block_input, segments, mix_gain, w_project, conv_taps, w_beta, w_gate, head_gain, w_output, ffn_gain, w_hidden_gate, w_hidden_up, w_hidden_down):
    residual = block_input.reshape(-1, D)
    normed = low(rms_scale(residual, low(mix_gain)))
    projected = low_back(low(matmul(normed, low(w_project))))
    logits = matmul(normed, low(w_beta))
    gate = low_back(matmul(normed, low(w_gate)))
    mixed = jax.vmap(short_conv, in_axes=(0, 0, None))(projected.reshape(ROWS, ROW_LEN, 3 * D), segments, low(conv_taps))
    active = jax.nn.silu(mixed)
    query = unit_rows(active[..., :D].reshape(ROWS, ROW_LEN, H, HEAD))
    key = unit_rows(active[..., D:2 * D].reshape(ROWS, ROW_LEN, H, HEAD))
    value = active[..., 2 * D:].reshape(ROWS, ROW_LEN, H, HEAD)
    strength = jax.nn.sigmoid(logits).reshape(ROWS, ROW_LEN, H)
    previous = jnp.concatenate([segments[:, :1], segments[:, :-1]], 1)
    start = (segments != previous).astype(jnp.float32)
    recalled = jax.vmap(delta_row)(query, key, value, strength, start)
    gate_heads = gate.reshape(ROWS, ROW_LEN, H, HEAD)
    scaled = head_scale(recalled, low(head_gain).reshape(H, HEAD)) * jax.nn.silu(gate_heads)
    branch = low_back(matmul(low(scaled.reshape(-1, D)), low(w_output)))
    middle = residual + branch
    normed_two = low(rms_scale(middle, low(ffn_gain)))
    gate_two = low_back(matmul(normed_two, low(w_hidden_gate)))
    up_two = low_back(matmul(normed_two, low(w_hidden_up)))
    hidden = low(jax.nn.silu(gate_two) * up_two)
    result = middle + low_back(matmul(hidden, low(w_hidden_down)))
    return result.reshape(ROWS, ROW_LEN, D)

def reference(block_input, segments, mix_gain, w_project, conv_taps, w_beta, w_gate, head_gain, w_output, ffn_gain, w_hidden_gate, w_hidden_up, w_hidden_down, cotangent):

    def forward(*floats):
        return layer(floats[0], segments, *floats[1:])
    primals = (block_input.astype(jnp.float32), mix_gain, w_project, conv_taps, w_beta, w_gate, head_gain, w_output, ffn_gain, w_hidden_gate, w_hidden_up, w_hidden_down)
    result, pullback = jax.vjp(forward, *primals)
    grads = pullback(cotangent.astype(jnp.float32))
    return (result.astype(jnp.bfloat16), grads[0], grads[1], grads[2], grads[3], grads[4], grads[5], grads[6], grads[7], grads[8], grads[9], grads[10], grads[11])
```

```python
import functools

import jax
import jax.numpy as jnp
from jax import lax
from jax.experimental import pallas as pl
from jax.experimental.pallas import tpu as pltpu
from jax.sharding import PartitionSpec as P

D = 2048
H = 16
HEAD = 128
CONV = 4
WIDTH = 8


EPS = 1e-06
HEAD_EPS = 0.01
HIGH = lax.Precision.HIGHEST
LOW = jnp.bfloat16
FULL = jnp.float32


def rms_scale(values, gain):
    return values * lax.rsqrt(jnp.mean(values * values, axis=-1, keepdims=True) + EPS) * gain


def dot_low(left, right):
    return jnp.dot(left, right, preferred_element_type=FULL)


def dot_left_t(left, right):
    return lax.dot_general(left, right, (((0,), (0,)), ((), ())), preferred_element_type=FULL)


def dot_right_t(left, right):
    return lax.dot_general(left, right, (((1,), (1,)), ((), ())), preferred_element_type=FULL)


def bits_of(count):
    return [1 << place for place in range(count.bit_length() - 1)]


def swap(values, axis, bit):
    return lax.ppermute(values, axis, [(i, i ^ bit) for i in range(lax.axis_size(axis))])


def grow(values, axis, bit, dim):
    upper = ((lax.axis_index(axis) & bit) != 0).astype(jnp.int32)
    other = swap(values, axis, bit)
    shape = values.shape[:dim] + (2,) + values.shape[dim:]
    own = lax.broadcasted_iota(jnp.int32, shape, dim) == upper
    both = jnp.where(own, jnp.expand_dims(values, dim), jnp.expand_dims(other, dim))
    return both.reshape(values.shape[:dim] + (2 * values.shape[dim],) + values.shape[dim + 1 :])


def halve(values, axis, bit, dim, waited=()):
    upper = ((lax.axis_index(axis) & bit) != 0).astype(jnp.int32)
    kept = lax.dynamic_index_in_dim(values, upper, dim, True)
    sent = lax.dynamic_index_in_dim(values, 1 - upper, dim, True)
    sent = sent.astype(LOW)
    return kept.astype(FULL) + swap(tie(sent, *waited) if waited else sent, axis, bit).astype(FULL)


def tie(values, *others):
    leaves, tree = jax.tree.flatten(values)
    waited = jax.tree.leaves(others)
    anywhere = pl.BlockSpec(memory_space=pl.ANY)
    passed = pl.pallas_call(
        lambda *refs: None,
        out_shape=[jax.ShapeDtypeStruct(leaf.shape, leaf.dtype) for leaf in leaves],
        in_specs=[anywhere] * (len(leaves) + len(waited)),
        out_specs=[anywhere] * len(leaves),
        input_output_aliases={at: at for at in range(len(leaves))},
        cost_estimate=pl.CostEstimate(flops=1024, bytes_accessed=1024, transcendentals=0),
    )(*leaves, *waited)
    return jax.tree.unflatten(tree, passed)


def hint(values, *others):
    return lax.optimization_barrier((values, *others))[0]


def turned_about(values, axis, unit, count, dim):
    place = lax.axis_index(axis) // unit
    shape = values.shape
    for bit in bits_of(count):
        split = values.reshape(shape[:dim] + (count // (2 * bit), 2, bit) + shape[dim + 1 :])
        flipped = jnp.flip(split, dim + 1)
        values = jnp.where((place & bit) != 0, flipped, split).reshape(shape)
    return values


def fiber_order(values, width):
    dp, cubes = lax.axis_size("dp"), lax.axis_size("seq") // width
    split = values.reshape(values.shape[:-1] + (dp, cubes, -1))
    dim = values.ndim - 1
    split = turned_about(split, "dp", 1, dp, dim)
    return turned_about(split, "seq", width, cubes, dim + 1).reshape(values.shape)


def near_gather(values, axis, unit, count):
    values = values[None]
    for bit in bits_of(count):
        values = jnp.concatenate([values, swap(values, axis, bit * unit)], 0)
    return values


def near_sum(values, axis, unit, count, waited=()):
    for bit in reversed(bits_of(count)):
        sent = values[bit:].astype(LOW)
        sent = swap(tie(sent, *waited) if waited else sent, axis, bit * unit)
        values = values[:bit].astype(FULL) + sent.astype(FULL)
    return values[0]


def cube_turn(values, width):
    seq = lax.axis_size("seq")
    groups = [list(range(first, first + width)) for first in range(0, seq, width)]
    return lax.all_to_all(values, "seq", 0, 0, axis_index_groups=groups, tiled=True)


def gather_all(values):
    count = lax.axis_size("dp") * lax.axis_size("seq")
    rows = jnp.broadcast_to(values[None], (count,) + values.shape)
    return lax.all_to_all(rows, ("dp", "seq"), 0, 0, tiled=True)


def sum_all(values):
    return jnp.sum(lax.all_to_all(values, ("dp", "seq"), 0, 0, tiled=True), axis=0)


def column_parts(columns, count):
    tiles = columns // 128
    edges = [128 * ((tiles * part) // count) for part in range(count + 1)]
    edges[-1] = columns
    return list(zip(edges[:-1], edges[1:]))


def cube_orders(width, parts):
    places = list(range(width.bit_length() - 1))
    if parts == 2 and len(places) > 2:
        return [places[1:] + places[:1], places[2:] + places[:2]]
    if parts == 3:
        return [places[start:] + places[:start] for start in range(len(places))] or [[]]
    return ([places[::-1], places[-1:] + places[:-1]] if len(places) > 2 else [places[::-1]])[:parts]


def cube_open(values, width, parts):
    rows, columns = values.shape
    orders = cube_orders(width, parts)
    cut = column_parts(columns, len(orders))
    return [values[:, low:high].reshape([1] * len(orders[0]) + [rows, high - low]) for low, high in cut]


def cube_step(blocks, width, parts, phase):
    orders = cube_orders(width, parts)
    depth = len(orders[0])
    return [
        grow(block, "seq", 1 << order[phase], depth - 1 - order[phase])
        for order, block in zip(orders, blocks)
    ]


def cube_close(blocks):
    return jnp.concatenate([block.reshape(-1, block.shape[-1]) for block in blocks], 1)


def cube_gather(values, width, parts):
    lead, (rows, columns) = values.shape[:-2], values.shape[-2:]
    orders = cube_orders(width, parts)
    depth = len(orders[0])
    done = []
    for order, (low, high) in zip(orders, column_parts(columns, len(orders))):
        block = values[..., low:high].reshape([1] * depth + list(values.shape[:-1]) + [high - low])
        for place in order:
            block = grow(block, "seq", 1 << place, depth - 1 - place)
        block = jnp.moveaxis(block.reshape((width,) + lead + (rows, high - low)), 0, -3)
        done.append(block.reshape(lead + (width * rows, high - low)))
    return jnp.concatenate(done, -1)


def cube_sum(values, width):
    blocks = values.astype(LOW).reshape((width, values.shape[0] // width) + values.shape[1:])
    return jnp.sum(cube_turn(blocks, width).astype(FULL), axis=0)


def cube_sum_by_axes(left, right, dot, width):
    rows = left.shape[0]
    orders = cube_orders(width, 2)
    depth = len(orders[0])
    done = []
    for order, part in zip(orders, right):
        block = dot(left, part)
        columns = block.shape[1]
        block = block.reshape([2] * depth + [rows // width, columns])
        for place in reversed(order):
            block = halve(block, "seq", 1 << place, depth - 1 - place)
        done.append(block.reshape(rows // width, columns))
    return jnp.concatenate(done, 1)


def fiber_gather_seq(values, width):
    values = values[None]
    for bit in bits_of(lax.axis_size("seq") // width):
        values = grow(values, "seq", bit * width, 0)
    return values


def chip_gather(values):
    for bit in bits_of(lax.axis_size("dp")):
        values = grow(values, "dp", bit, 0)
    return values


def chip_sum(values):
    rest = values.shape[1:]
    for bit in reversed(bits_of(lax.axis_size("dp"))):
        values = halve(values.reshape((2, -1) + rest), "dp", bit, 0)[0]
    return values


def far_sum(values, width, waited=()):
    rest = values.shape[1:]
    for bit in reversed(bits_of(lax.axis_size("seq") // width)):
        values = halve(values.reshape((2, -1) + rest), "seq", bit * width, 0, waited)[0]
    return values.reshape(rest)


CHUNK = 128
MICRO = 1 << 30
SPAN = 8
RIM = 16


def split(values):
    high = values.astype(LOW)
    return (high, (values - high.astype(FULL)).astype(LOW))


def mul(left, right):
    return jnp.dot(
        jnp.concatenate([left[0], left[1], left[0]], 1),
        jnp.concatenate([right[0], right[0], right[1]], 0),
        preferred_element_type=FULL,
    )


def mul_t(left, right):
    return lax.dot_general(
        jnp.concatenate([left[0], left[1], left[0]], 1),
        jnp.concatenate([right[0], right[0], right[1]], 1),
        (((1,), (1,)), ((), ())),
        preferred_element_type=FULL,
    )


def grid_index(dim):
    return lax.broadcasted_iota(jnp.int32, (CHUNK, CHUNK), dim)


def row_sum(values):
    return jnp.sum(values, axis=1, keepdims=True)


def here_rows(chunk):
    return pl.ds(pl.multiple_of(chunk * CHUNK + RIM, SPAN), CHUNK)


def conv_part(mix_ref, taps_ref, cols, chunk, low):
    start = pl.multiple_of(chunk * CHUNK + RIM - SPAN, SPAN)
    rows = mix_ref[pl.ds(start, CHUNK + SPAN), low : low + HEAD].astype(LOW).astype(FULL)
    total = jnp.zeros((CHUNK, HEAD), FULL)
    terms = []
    for tap in range(CONV):
        back = CONV - 1 - tap
        moved = rows if back == 0 else pltpu.roll(rows, back, 0)
        term = moved[SPAN:] * cols[:, tap : tap + 1]
        terms.append(term)
        total = total + taps_ref[tap : tap + 1, low : low + HEAD] * term
    return (total, terms)


def unit_part(values):
    scale = lax.rsqrt(row_sum(values * values) + EPS)
    return (values * scale, scale)


def prep_kernel(heads, deep, mix_ref, taps_ref, cols_ref, seg_ref, *outs):
    q_ref, k_ref, uk_ref, uv_ref, inv_ref, att_ref, map_ref, add_ref, far_ref, end_ref = outs
    mine = heads * HEAD
    chunks = seg_ref.shape[0]
    group = 2 if chunks % 2 == 0 else 1
    i_at, j_at = grid_index(0), grid_index(1)
    apart = i_at ^ j_at
    eye = (i_at == j_at).astype(FULL)

    def some(step, carry):
        work = []
        for offset in range(group):
            chunk = step * group + offset
            cols = cols_ref[pl.ds(pl.multiple_of(chunk * CHUNK, CHUNK), CHUNK), :]
            same = cols[:, 4:5] == seg_ref[chunk]
            lower = (same & (j_at < i_at)).astype(FULL)
            inclusive = (same & (j_at <= i_at)).astype(FULL)
            carried, ending = cols[:, 5:6], cols[:, 6:7]
            for head in range(heads):
                at = chunk * heads + head
                parts = [
                    jax.nn.silu(
                        conv_part(mix_ref, taps_ref, cols, chunk, part * mine + head * HEAD)[0]
                    )
                    for part in range(3)
                ]
                query, key = unit_part(parts[0])[0], unit_part(parts[1])[0]
                last = mix_ref[here_rows(chunk), 4 * mine : 4 * mine + HEAD]
                weight = jax.nn.sigmoid(last[:, head : head + 1])
                q_ref[at] = query
                k_ref[at] = key
                key_s, query_s = split(key), split(query)
                both = tuple(jnp.concatenate([a, b], 0) for a, b in zip(key_s, query_s))
                grams = mul_t(both, key_s)
                att_ref[at] = grams[CHUNK:] * inclusive
                below = weight * grams[:CHUNK] * lower
                work.append([at, key, parts[2], weight, carried, ending, below])
        inverses = [eye - jnp.where(apart == 1, item[6], 0.0) for item in work]
        level = 1
        while (1 << level) < CHUNK:
            next_inverses = []
            for item, inverse in zip(work, inverses):
                inverse_s = split(inverse)
                block = split(jnp.where((apart >> level) == 1, item[6], 0.0))
                inner = split(mul(inverse_s, block))
                next_inverses.append(inverse - mul(inner, inverse_s))
            inverses = next_inverses
            level += 1
        for item, inverse in zip(work, inverses):
            at, key, value, weight, carried, ending, below = item
            inv_ref[at] = inverse
            right = jnp.concatenate([(weight * carried) * key, weight * value], 1)
            solved = mul(split(inverse), split(right))
            uk_ref[at] = solved[:, :HEAD]
            uv_ref[at] = solved[:, HEAD:]
            turned = mul(split((key * ending).T), split(solved))
            map_ref[at] = carried[CHUNK - 1 :] * eye - turned[:, :HEAD]
            add_ref[at] = turned[:, HEAD:]
        return carry

    lax.fori_loop(0, chunks // group, some, 0)

    end_ref[...] = jnp.zeros_like(end_ref)
    for head in range(heads):
        far_ref[head] = eye

    def chain(chunk, carry):
        for head in range(heads):
            at = chunk * heads + head
            step = split(map_ref[at])
            end_ref[head] = mul(step, split(end_ref[head])) + add_ref[at]
            if deep:
                far_ref[head] = mul(step, split(far_ref[head]))
        return carry

    lax.fori_loop(0, chunks, chain, 0)


def run_kernel(heads, mix_ref, cols_ref, gain_ref, q_ref, uk_ref, uv_ref, att_ref, map_ref, add_ref, state_ref, *outs):
    p_ref, delta_ref, out_ref, scaled_ref, now_ref = outs
    mine = heads * HEAD
    chunks = p_ref.shape[0] // heads
    now_ref[...] = state_ref[...]

    def one(chunk, carry):
        start = pl.multiple_of(chunk * CHUNK, CHUNK)
        carried = cols_ref[pl.ds(start, CHUNK), :][:, 5:6]
        for head in range(heads):
            at = chunk * heads + head
            state = now_ref[head]
            p_ref[at] = state
            state_s = split(state)
            now_ref[head] = mul(split(map_ref[at]), state_s) + add_ref[at]
            both = split(jnp.concatenate([uk_ref[at], q_ref[at]], 0))
            seen = mul(both, state_s)
            delta = uv_ref[at] - seen[:CHUNK]
            delta_ref[at] = delta
            output = carried * seen[CHUNK:] + mul(split(att_ref[at]), split(delta))
            out_ref[at] = output
            low = 3 * mine + head * HEAD
            gate = mix_ref[here_rows(chunk), low : low + HEAD]
            scale = lax.rsqrt(row_sum(output * output) / HEAD + HEAD_EPS)
            gain = gain_ref[:, head * HEAD : (head + 1) * HEAD]
            scaled = output * scale * gain * jax.nn.silu(gate)
            scaled_ref[pl.ds(start, CHUNK), head * HEAD : (head + 1) * HEAD] = scaled.astype(LOW)
        return carry

    lax.fori_loop(0, chunks, one, 0)


def silu_slope(values):
    gate = jax.nn.sigmoid(values)
    return gate * (1.0 + values * (1.0 - gate))


def back_kernel(heads, mix_ref, cols_ref, gain_ref, q_ref, uk_ref, att_ref, map_ref, out_ref, grad_ref, *outs):
    dout_ref, first_ref, term_ref, dgate_ref, end_ref = outs
    mine = heads * HEAD
    chunks = out_ref.shape[0] // heads
    end_ref[...] = jnp.zeros_like(end_ref)

    def one(step, carry):
        chunk = chunks - 1 - step
        start = pl.multiple_of(chunk * CHUNK, CHUNK)
        carried = cols_ref[pl.ds(start, CHUNK), :][:, 5:6]
        for head in range(heads):
            at = chunk * heads + head
            here = slice(head * HEAD, (head + 1) * HEAD)
            low = 3 * mine + head * HEAD
            gate = mix_ref[here_rows(chunk), low : low + HEAD]
            output = out_ref[at]
            grad = grad_ref[pl.ds(start, CHUNK), here].astype(FULL)
            gain = gain_ref[:, here]
            scale = lax.rsqrt(row_sum(output * output) / HEAD + HEAD_EPS)
            unit = output * scale
            opened = jax.nn.silu(gate)
            dgate_ref[pl.ds(start, CHUNK), here] = (grad * unit * gain * silu_slope(gate)).astype(LOW)
            inner = grad * gain * opened
            dout = scale * (inner - unit * (row_sum(inner * unit) / HEAD))
            dout_ref[at] = dout
            first = mul(split(att_ref[at].T), split(dout))
            first_ref[at] = first
            left = split(jnp.concatenate([q_ref[at].T, uk_ref[at].T], 1))
            term = mul(left, split(jnp.concatenate([carried * dout, -first], 0)))
            term_ref[at] = term
            end_ref[head] = mul(split(map_ref[at].T), split(end_ref[head])) + term
        return carry

    lax.fori_loop(0, chunks, one, 0)


def pull_kernel(heads, mix_ref, taps_ref, cols_ref, seg_ref, *rest):
    (q_ref, k_ref, inv_ref, att_ref, map_ref, p_ref, delta_ref) = rest[:7]
    (dout_ref, first_ref, term_ref, dgate_ref, leave_ref) = rest[7:12]
    gmix_ref, tail_ref, edge_ref, dtaps_ref, now_ref, next_ref = rest[12:]
    gmix_ref[:RIM] = jnp.zeros((RIM, gmix_ref.shape[1]), LOW)
    mine = heads * HEAD
    chunks = seg_ref.shape[0]
    i_at, j_at = grid_index(0), grid_index(1)
    now_ref[...] = leave_ref[...]
    next_ref[...] = jnp.zeros_like(next_ref)
    dtaps_ref[...] = jnp.zeros_like(dtaps_ref)

    def one(step, carry):
        chunk = chunks - 1 - step
        start = pl.multiple_of(chunk * CHUNK, CHUNK)
        cols_far = cols_ref[pl.ds(start, CHUNK + SPAN), :]
        cols = cols_far[:CHUNK]
        same = cols[:, 4:5] == seg_ref[chunk]
        lower = (same & (j_at < i_at)).astype(FULL)
        inclusive = (same & (j_at <= i_at)).astype(FULL)
        carried, ending = cols[:, 5:6], cols[:, 6:7]
        last = mix_ref[here_rows(chunk), 4 * mine : 4 * mine + HEAD]
        dlast = jnp.zeros((CHUNK, HEAD), FULL)
        for head in range(heads):
            at = chunk * heads + head
            lows = [part * mine + head * HEAD for part in range(3)]
            mixed = [conv_part(mix_ref, taps_ref, cols, chunk, low) for low in lows]
            query, query_scale = unit_part(jax.nn.silu(mixed[0][0]))
            key, key_scale = unit_part(jax.nn.silu(mixed[1][0]))
            value = jax.nn.silu(mixed[2][0])
            weight = jax.nn.sigmoid(last[:, head : head + 1])
            key_s = split(key)
            leave = now_ref[head]
            leave_s = split(leave)
            now_ref[head] = mul(split(map_ref[at].T), leave_s) + term_ref[at]
            ddelta = first_ref[at] + mul(split(key * ending), leave_s)
            solved = mul(split(inv_ref[at].T), split(ddelta))
            delta_s = split(delta_ref[at])
            dout = dout_ref[at]
            ends = split(jnp.concatenate([solved, dout], 0))
            by_state = mul_t(ends, split(p_ref[at]))
            by_delta = mul_t(ends, delta_s)
            dright = -by_state[:CHUNK]
            dsystem = -by_delta[:CHUNK] * lower
            datt = by_delta[CHUNK:] * inclusive
            dquery = carried * by_state[CHUNK:] + mul(split(datt), key_s)
            gram = mul_t(key_s, key_s)
            dgram = weight * dsystem
            left = split(jnp.concatenate([datt.T, dgram + dgram.T], 1))
            right = tuple(jnp.concatenate([a, b], 0) for a, b in zip(split(query), key_s))
            dkey = mul(left, right) + (weight * carried) * dright
            dkey = dkey + ending * mul_t(delta_s, leave_s)
            dvalue = weight * solved
            dweight = row_sum(solved * value + carried * dright * key + dsystem * gram)
            dlogit = dweight * weight * (1.0 - weight)
            dlast = jnp.where(j_at == head, dlogit, dlast)
            dactive = [
                query_scale * (dquery - query * row_sum(dquery * query)),
                key_scale * (dkey - key * row_sum(dkey * key)),
                dvalue,
            ]
            for part, low in enumerate(lows):
                total, terms = mixed[part]
                dtotal = dactive[part] * silu_slope(total)
                here = slice(low, low + HEAD)
                far = jnp.concatenate([dtotal, next_ref[:, here]], 0)
                near = jnp.concatenate([jnp.zeros((SPAN, HEAD), FULL), dtotal[:SPAN]], 0)
                next_ref[:, here] = dtotal[:SPAN]
                dproj = jnp.zeros((CHUNK, HEAD), FULL)
                edge = jnp.zeros((SPAN, HEAD), FULL)
                zero = jnp.zeros((SPAN, 1), FULL)
                for tap in range(CONV):
                    back = CONV - 1 - tap
                    tap_row = taps_ref[tap : tap + 1, here]
                    dtaps_ref[tap : tap + 1, here] += jnp.sum(dtotal * terms[tap], axis=0, keepdims=True)
                    spread = far * cols_far[:, tap : tap + 1]
                    near_mask = jnp.concatenate([zero, cols[:SPAN, tap : tap + 1]], 0)
                    close = near * near_mask
                    if back > 0:
                        spread = pltpu.roll(spread, CHUNK + SPAN - back, 0)
                        close = pltpu.roll(close, 2 * SPAN - back, 0)
                        edge = edge + tap_row * close[:SPAN]
                    dproj = dproj + tap_row * spread[:CHUNK]
                gmix_ref[here_rows(chunk), here] = dproj.astype(LOW)
                edge_ref[:, here] = edge

                @pl.when(step == 0)
                def _():
                    tail_ref[:, here] = dproj[CHUNK - SPAN :]

        gmix_ref[here_rows(chunk), 3 * mine : 4 * mine] = dgate_ref[pl.ds(start, CHUNK), :]
        gmix_ref[here_rows(chunk), 4 * mine : 4 * mine + HEAD] = dlast.astype(LOW)
        return carry

    lax.fori_loop(0, chunks, one, 0)
    gap = jnp.zeros((RIM - SPAN, 3 * mine), FULL)
    gmix_ref[:RIM, : 3 * mine] = jnp.concatenate([gap, edge_ref[...]], 0).astype(LOW)


def on_chip(body, shapes, scratch, flops, waited, *operands):
    whole = pl.BlockSpec(memory_space=pltpu.VMEM)
    anywhere = pl.BlockSpec(memory_space=pl.ANY)
    used, spare = len(operands), len(waited)
    return pl.pallas_call(
        lambda *refs: body(*refs[:used], *refs[used + spare :]),
        out_shape=shapes,
        in_specs=[whole] * used + [anywhere] * spare,
        out_specs=[whole] * len(shapes),
        scratch_shapes=list(scratch),
        compiler_params=pltpu.CompilerParams(vmem_limit_bytes=56 * 1024 * 1024),
        cost_estimate=pl.CostEstimate(flops=flops, bytes_accessed=20 * 1024 * 1024, transcendentals=0),
    )(*operands, *waited)


def squares(*counts):
    return tuple(jax.ShapeDtypeStruct((count, HEAD, HEAD), FULL) for count in counts)


def delta_prep(heads, deep, mix, taps, cols, segs, waited):
    each = segs.shape[0] * heads
    shapes = squares(*[each] * 8, heads, heads)
    body = functools.partial(prep_kernel, heads, deep)
    return on_chip(body, shapes, (), 30 * MICRO, waited, mix, taps, cols, segs)


def delta_run(heads, mix, cols, gain, prepared, state, waited):
    q, k, uk, uv, inv, att, step, add = prepared
    each = q.shape[0]
    count = each // heads * CHUNK
    shapes = squares(each, each, each) + (jax.ShapeDtypeStruct((count, heads * HEAD), LOW),)
    body = functools.partial(run_kernel, heads)
    scratch = [pltpu.VMEM((heads, HEAD, HEAD), FULL)]
    flops = 11 * MICRO
    return on_chip(
        body, shapes, scratch, flops, waited, mix, cols, gain, q, uk, uv, att, step, add, state
    )


def delta_back(heads, mix, cols, gain, prepared, output, grad, waited):
    q, k, uk, uv, inv, att, step, add = prepared
    each = q.shape[0]
    count = each // heads * CHUNK
    mine = heads * HEAD
    shapes = squares(each, each, each) + (
        jax.ShapeDtypeStruct((count, mine), LOW),
    ) + squares(heads)
    body = functools.partial(back_kernel, heads)
    flops = 12 * MICRO
    return on_chip(
        body, shapes, (), flops, waited, mix, cols, gain, q, uk, att, step, output, grad
    )


def delta_pull(heads, mix, taps, cols, segs, prepared, states, delta, backs, leaving, waited):
    q, k, uk, uv, inv, att, step, add = prepared
    dout, first, term, dgate = backs
    mine = heads * HEAD
    shapes = (
        jax.ShapeDtypeStruct(mix.shape, LOW),
        jax.ShapeDtypeStruct((SPAN, 3 * mine), FULL),
        jax.ShapeDtypeStruct((SPAN, 3 * mine), FULL),
        jax.ShapeDtypeStruct((SPAN, 3 * mine), FULL),
    )
    body = functools.partial(pull_kernel, heads)
    scratch = [pltpu.VMEM((heads, HEAD, HEAD), FULL), pltpu.VMEM((SPAN, 3 * mine), FULL)]
    flops = 30 * MICRO
    return on_chip(
        body, shapes, scratch, flops, waited, mix, taps, cols, segs, q, k, inv, att, step, states, delta, dout, first, term, dgate, leaving
    )


def swiglu(gate_two, up_two):
    return jax.nn.silu(gate_two) * up_two


def local(
    block_input,
    segments,
    mix_gain,
    w_project,
    conv_taps,
    w_beta,
    w_gate,
    head_gain,
    w_output,
    ffn_gain,
    w_hidden_gate,
    w_hidden_up,
    w_hidden_down,
    cotangent,
):
    dp, seq = lax.axis_size("dp"), lax.axis_size("seq")
    width = min(WIDTH, seq & -seq)
    cubes = seq // width
    everyone = dp * seq
    fiber = dp * cubes
    both = ("dp", "seq")
    row_at, chip_at = lax.axis_index("dp"), lax.axis_index("seq")
    me = chip_at % width
    cube_at = chip_at // width
    heads = H // width
    mine = heads * HEAD
    rows = w_project.shape[0]
    tokens = block_input.shape[1]
    count = tokens * width
    units = w_hidden_down.shape[0]
    hidden_mine = fiber * units

    taps_each = conv_taps.shape[1]
    packed = jnp.concatenate(
        [
            mix_gain.astype(LOW),
            head_gain.astype(LOW),
            ffn_gain.astype(LOW),
            conv_taps.astype(LOW).reshape(-1),
            segments[0].astype(LOW),
        ]
    )
    mixer_pad = -(mine * 4 + heads) % 128
    mixer_low = jnp.concatenate(
        [
            jnp.swapaxes(w_project.reshape(rows, 3, width, mine), 1, 2).reshape(rows, width, 3 * mine),
            w_gate.reshape(rows, width, mine),
            w_beta.reshape(rows, width, heads),
            jnp.zeros((rows, width, mixer_pad), FULL),
        ],
        -1,
    ).astype(LOW)
    mixer_turned = cube_turn(jnp.swapaxes(mixer_low, 0, 1), width)
    small = gather_all(packed)
    gain_one = small[:, :rows].reshape(D).astype(FULL)
    gain_head = small[:, rows : 2 * rows].reshape(D).astype(FULL)
    gain_two = small[:, 2 * rows : 3 * rows].reshape(D).astype(FULL)
    taps_full = small[:, 3 * rows : 3 * rows + CONV * taps_each].reshape(everyone, CONV, taps_each)
    taps_full = jnp.swapaxes(taps_full, 0, 1).reshape(CONV, 3, width, mine).astype(FULL)
    taps_mine = lax.dynamic_index_in_dim(taps_full, me, 2, False).reshape(CONV, 3 * mine)
    gain_mine = lax.dynamic_index_in_dim(gain_head.reshape(width, heads, HEAD), me, 0, False)
    seg_all = small[:, 3 * rows + CONV * taps_each :].astype(jnp.int32).reshape(dp, seq * tokens)
    seg_row = lax.dynamic_index_in_dim(seg_all, row_at, 0, False)
    ext_seg = lax.dynamic_slice_in_dim(
        jnp.concatenate([jnp.zeros((CONV - 1,), jnp.int32), seg_row]),
        cube_at * count,
        count + CONV - 1,
    )
    seg_mine = ext_seg[CONV - 1 :]
    tokens_in = jnp.concatenate([fiber_order(block_input, width), cotangent], 0)
    pair = cube_gather(tokens_in, width, 2)
    x_cube, g_out = pair[0], pair[1]
    ahead = [(i, i + width) for i in range(seq - width)]
    behind = [(i + width, i) for i in range(seq - width)]
    rim = lax.ppermute(fiber_order(x_cube[count - RIM :], width), "seq", ahead)
    x_more = jnp.concatenate([fiber_order(rim, width), x_cube], 0)
    mixer_far = near_gather(mixer_turned, "seq", width, cubes)
    mixer_w = near_gather(mixer_far, "dp", 1, dp).reshape(D, -1)

    hgate_late, hup_late = hint((w_hidden_gate, w_hidden_up), mixer_turned)

    def by_units(weight):
        split = weight.astype(LOW).reshape(rows, dp, cubes, width, units)
        return jnp.transpose(split, (3, 0, 1, 2, 4)).reshape(width, rows, hidden_mine)

    ffn_low = jnp.concatenate([by_units(hgate_late), by_units(hup_late)], -1)
    ffn_turned = cube_turn(ffn_low, width)
    ffn_far = near_gather(hint(ffn_turned, mixer_far), "seq", width, cubes)

    residual = block_input[0].astype(FULL)
    normed_own, mix_pull = jax.vjp(lambda v: rms_scale(v, gain_one), residual)
    normed = rms_scale(x_more.astype(FULL), fiber_order(gain_one, width)).astype(LOW)
    mixed_in = dot_low(normed, mixer_w)
    out_low, down_low, mixed_in = lax.optimization_barrier(
        (w_output.astype(LOW), w_hidden_down.astype(LOW), mixed_in)
    )
    out_far = near_gather(out_low, "seq", width, cubes)
    out_spread = jnp.broadcast_to(out_far[None], (width,) + out_far.shape)
    out_near = cube_turn(out_spread, width).reshape(D // dp, D)
    chunks = count // CHUNK
    seg_chunks = seg_mine.reshape(chunks, CHUNK)
    before = jnp.concatenate([ext_seg[CONV - 2 : CONV - 1], seg_chunks[:-1, -1]], 0)
    columns = [ext_seg[tap : tap + count] == seg_mine for tap in range(CONV)]
    columns.append(seg_mine)
    columns.append((seg_chunks == before[:, None]).reshape(count))
    columns.append((seg_chunks == seg_chunks[:, -1:]).reshape(count))
    columns.append(jnp.zeros((count,), FULL))
    cols = jnp.stack([column.astype(FULL) for column in columns], 1)
    cols = jnp.pad(cols, ((0, SPAN), (0, 0)))
    segs = seg_chunks.astype(FULL)[:, None, :]
    gain_row = gain_mine.reshape(1, mine)
    prepared = delta_prep(heads, cubes > 2, mixed_in, taps_mine, cols, segs, ())
    far, end = prepared[8:]
    prepared = prepared[:8]
    state_in = jnp.zeros((heads, HEAD, HEAD), FULL)
    for hop in range(cubes - 1):
        out = end
        if hop > 0:
            out = end + jnp.einsum("hij,hjk->hik", far, state_in, precision=HIGH)
        state_in = lax.ppermute(out, "seq", ahead)
    states, delta, recalled, scaled = delta_run(
        heads, mixed_in, cols, gain_row, prepared, state_in, ()
    )
    ffn_w = near_gather(ffn_far, "dp", 1, dp).reshape(D, 2 * hidden_mine)
    out_parts = [out_near]
    for bit in bits_of(dp):
        out_parts = out_parts + [swap(part, "dp", bit) for part in out_parts]
    scaled_own = jnp.swapaxes(cube_turn(scaled.reshape(width, tokens, mine), width), 0, 1)
    down_w = chip_gather(fiber_gather_seq(down_low, width)).reshape(hidden_mine, D)
    scaled_own = fiber_order(scaled_own.reshape(tokens, D), width)
    scaled_own = jnp.swapaxes(scaled_own.reshape(tokens, dp, cubes, width, rows), 2, 3)
    scaled_own = scaled_own.reshape(tokens, dp, D // dp)
    middle = residual
    for at, part in enumerate(out_parts):
        middle = middle + dot_low(scaled_own[:, at], part)

    normed_two_f, ffn_pull = jax.vjp(lambda v: rms_scale(v, gain_two), middle)
    normed_two = cube_gather(fiber_order(normed_two_f.astype(LOW), width), width, 3)
    both_two = dot_low(normed_two, ffn_w)
    gate_two, up_two = both_two[:, :hidden_mine], both_two[:, hidden_mine:]
    hidden_f, glu_pull = jax.vjp(swiglu, gate_two, up_two)
    hidden = hidden_f.astype(LOW)
    grad_hidden = dot_right_t(g_out, down_w)
    grad_gate_two, grad_up_two = glu_pull(grad_hidden)
    grad_both = jnp.concatenate([grad_gate_two.astype(LOW), grad_up_two.astype(LOW)], 1)
    pulled = dot_right_t(grad_both, ffn_w).astype(LOW)
    grad_normed_two = fiber_order(cube_sum(pulled, width), width)
    grad_down = chip_sum(dot_left_t(hidden, g_out).reshape(fiber, units, D))
    grad_ffn = dot_left_t(normed_two, grad_both).reshape(dp, cubes, width, rows, -1)
    grad_ffn = near_sum(grad_ffn, "dp", 1, dp)
    grad_normed_two, grad_ffn, grad_down = lax.optimization_barrier(
        (grad_normed_two, grad_ffn, grad_down)
    )
    grad_ffn = [grad_ffn[..., :hidden_mine], grad_ffn[..., hidden_mine:]]
    (grad_middle,) = ffn_pull(grad_normed_two)
    grad_middle = grad_middle + cotangent[0].astype(FULL)
    grad_branch = grad_middle.astype(LOW)
    grad_scaled_own = jnp.stack([dot_right_t(grad_branch, part).astype(LOW) for part in out_parts], 1)
    grad_scaled_own = jnp.swapaxes(grad_scaled_own.reshape(tokens, dp, width, cubes, rows), 2, 3)
    grad_scaled_own = fiber_order(grad_scaled_own.reshape(tokens, D), width)

    grad_scaled = cube_turn(
        jnp.swapaxes(grad_scaled_own.reshape(tokens, width, mine), 0, 1), width
    ).reshape(count, mine)
    owners = []
    for row in range(dp):
        for chip in range(seq):
            block = (chip % width) * fiber + row * cubes + chip // width
            owners.append((row * seq + chip, block))
    groups = [list(range(first, first + width)) for first in range(0, seq, width)]
    branch_cube = lax.all_gather(grad_branch, "seq", axis_index_groups=groups, tiled=True)
    half = D // len(cube_orders(width, 2))
    down_parts = [down_w[:, at : at + half] for at in range(0, D, half)]
    result = middle + cube_sum_by_axes(tie(hidden, grad_branch), down_parts, dot_low, width)
    block_output = result.astype(LOW)[None]
    backs = delta_back(
        heads, mixed_in, cols, gain_row, prepared, recalled, grad_scaled, ()
    )
    end_back = backs[4]
    leaving = jnp.zeros((heads, HEAD, HEAD), FULL)
    for hop in range(cubes - 1):
        out = end_back
        if hop > 0:
            out = end_back + jnp.einsum("hji,hjk->hik", far, leaving, precision=HIGH)
        leaving = lax.ppermute(out, "seq", behind)
    grad_down = far_sum(grad_down, width, (leaving,))
    grad_hgate = near_sum(grad_ffn[0], "seq", width, cubes, (leaving,))
    grad_mixed, tail, edge, grad_taps = delta_pull(
        heads, mixed_in, taps_mine, cols, segs, prepared, states, delta, backs[:4], leaving,
        (),
    )
    grad_hup = near_sum(grad_ffn[1], "seq", width, cubes, (grad_hgate, leaving))
    grad_mixed = hint(grad_mixed, grad_hgate)
    grad_mixer = dot_left_t(normed, grad_mixed).reshape(dp, cubes, width, rows, -1)
    grad_mixer = near_sum(grad_mixer, "dp", 1, dp)
    from_next = lax.ppermute(edge.astype(LOW), "seq", behind).astype(FULL)
    grad_fixed = lax.dynamic_update_slice(
        grad_mixed[RIM:], (tail + from_next).astype(LOW), (count - SPAN, 0)
    )
    grad_taps = grad_taps[:CONV]
    mixer_parts = [mixer_w[at : at + half] for at in range(0, D, half)]
    grad_mixer = near_sum(grad_mixer, "seq", width, cubes, (grad_hup, grad_down)).astype(LOW)
    grad_normed = cube_sum_by_axes(grad_fixed, mixer_parts, dot_right_t, width)
    grad_normed = fiber_order(grad_normed, width)
    grad_oproj = chip_sum(dot_left_t(scaled, branch_cube).reshape(fiber, rows, D))
    grad_oproj = far_sum(grad_oproj, width)
    grad_oproj = lax.ppermute(grad_oproj.astype(LOW), both, owners).astype(FULL)
    grad_ffn = jnp.concatenate([grad_hgate.astype(LOW), grad_hup.astype(LOW)], -1)
    grad_ffn = cube_turn(tie(grad_ffn, block_output), width)
    taps_wide = lax.dynamic_update_index_in_dim(
        jnp.zeros((CONV, 3, width, mine), FULL), grad_taps.reshape(CONV, 3, mine), me, 2
    ).reshape(CONV, everyone, taps_each)
    taps_wide = jnp.swapaxes(taps_wide, 0, 1).reshape(everyone, CONV * taps_each)
    taps_own = sum_all(taps_wide)
    grad_mixer = cube_turn(tie(grad_mixer, grad_ffn, taps_own), width).astype(FULL)
    grad_ffn = grad_ffn.astype(FULL)

    def by_rows(grad):
        split = grad.reshape(width, rows, dp, cubes, units)
        return jnp.transpose(split, (1, 2, 3, 0, 4)).reshape(rows, -1)

    grad_hgate, grad_hup = by_rows(grad_ffn[..., :hidden_mine]), by_rows(grad_ffn[..., hidden_mine:])
    grad_mixer = jnp.swapaxes(grad_mixer, 0, 1)
    grad_wproj = jnp.swapaxes(grad_mixer[..., : 3 * mine].reshape(rows, width, 3, mine), 1, 2)
    grad_wproj = grad_wproj.reshape(rows, 3 * D)
    grad_wgate = grad_mixer[..., 3 * mine : 4 * mine].reshape(rows, D)
    grad_wbeta = grad_mixer[..., 4 * mine : 4 * mine + heads].reshape(rows, H)
    (grad_tokens,) = mix_pull(grad_normed)
    grad_input = (grad_tokens + grad_middle)[None]

    def gain_grad(gain, *pairs):
        terms = [row_sum(weight.astype(LOW).astype(FULL) * grad) for weight, grad in pairs]
        return sum(terms)[:, 0] / gain.astype(LOW).astype(FULL)

    grad_mgain = gain_grad(mix_gain, (w_project, grad_wproj), (w_gate, grad_wgate), (w_beta, grad_wbeta))
    grad_hgain = gain_grad(head_gain, (w_output, grad_oproj))
    grad_fgain = gain_grad(ffn_gain, (w_hidden_gate, grad_hgate), (w_hidden_up, grad_hup))
    return (
        block_output,
        grad_input,
        grad_mgain,
        grad_wproj,
        taps_own.reshape(CONV, taps_each),
        grad_wbeta,
        grad_wgate,
        grad_hgain,
        grad_oproj,
        grad_fgain,
        grad_hgate,
        grad_hup,
        grad_down,
    )


def solution(mesh):
    tokens = P("dp", "seq", None)
    vector = P(("dp", "seq"))
    matrix = P(("dp", "seq"), None)
    taps = P(None, ("dp", "seq"))
    in_specs = (tokens, P("dp", "seq"), vector, matrix, taps, matrix, matrix, vector, matrix)
    in_specs = in_specs + (vector, matrix, matrix, matrix, tokens)
    out_specs = (tokens, tokens, vector, matrix, taps, matrix, matrix, vector, matrix)
    out_specs = out_specs + (vector, matrix, matrix, matrix)
    return jax.shard_map(local, mesh=mesh, in_specs=in_specs, out_specs=out_specs, check_vma=False)
```

```python
import functools

import jax
import jax.numpy as jnp
from jax import lax
from jax.experimental import pallas as pl
from jax.experimental.pallas import tpu as pltpu
from jax.sharding import PartitionSpec as P

D = 2048
H = 16
HEAD = 128
CONV = 4
WIDTH = 8


EPS = 1e-06
HEAD_EPS = 0.01
HIGH = lax.Precision.HIGHEST
LOW = jnp.bfloat16
FULL = jnp.float32


def rms_scale(values, gain):
    return values * lax.rsqrt(jnp.mean(values * values, axis=-1, keepdims=True) + EPS) * gain


def dot_low(left, right):
    return jnp.dot(left, right, preferred_element_type=FULL)


def dot_left_t(left, right):
    return lax.dot_general(left, right, (((0,), (0,)), ((), ())), preferred_element_type=FULL)


def dot_right_t(left, right):
    return lax.dot_general(left, right, (((1,), (1,)), ((), ())), preferred_element_type=FULL)


def bits_of(count):
    return [1 << place for place in range(count.bit_length() - 1)]


def swap(values, axis, bit):
    return lax.ppermute(values, axis, [(i, i ^ bit) for i in range(lax.axis_size(axis))])


def grow(values, axis, bit, dim):
    upper = ((lax.axis_index(axis) & bit) != 0).astype(jnp.int32)
    other = swap(values, axis, bit)
    shape = values.shape[:dim] + (2,) + values.shape[dim:]
    own = lax.broadcasted_iota(jnp.int32, shape, dim) == upper
    both = jnp.where(own, jnp.expand_dims(values, dim), jnp.expand_dims(other, dim))
    return both.reshape(values.shape[:dim] + (2 * values.shape[dim],) + values.shape[dim + 1 :])


def halve(values, axis, bit, dim, waited=(), later=()):
    upper = ((lax.axis_index(axis) & bit) != 0).astype(jnp.int32)
    kept = lax.dynamic_index_in_dim(values, upper, dim, True)
    sent = lax.dynamic_index_in_dim(values, 1 - upper, dim, True)
    sent = sent.astype(LOW)
    come = swap(tie(sent, *waited) if waited else sent, axis, bit)
    return kept.astype(FULL) + (tie(come, *later) if later else come).astype(FULL)


def tie(values, *others):
    leaves, tree = jax.tree.flatten(values)
    waited = jax.tree.leaves(others)
    anywhere = pl.BlockSpec(memory_space=pl.ANY)
    passed = pl.pallas_call(
        lambda *refs: None,
        out_shape=[jax.ShapeDtypeStruct(leaf.shape, leaf.dtype) for leaf in leaves],
        in_specs=[anywhere] * (len(leaves) + len(waited)),
        out_specs=[anywhere] * len(leaves),
        input_output_aliases={at: at for at in range(len(leaves))},
        cost_estimate=pl.CostEstimate(flops=1024, bytes_accessed=1024, transcendentals=0),
    )(*leaves, *waited)
    return jax.tree.unflatten(tree, passed)


def hint(values, *others):
    return lax.optimization_barrier((values, *others))[0]


def turned_about(values, axis, unit, count, dim):
    place = lax.axis_index(axis) // unit
    shape = values.shape
    for bit in bits_of(count):
        split = values.reshape(shape[:dim] + (count // (2 * bit), 2, bit) + shape[dim + 1 :])
        flipped = jnp.flip(split, dim + 1)
        values = jnp.where((place & bit) != 0, flipped, split).reshape(shape)
    return values


def fiber_order(values, width):
    dp, cubes = lax.axis_size("dp"), lax.axis_size("seq") // width
    split = values.reshape(values.shape[:-1] + (dp, cubes, -1))
    dim = values.ndim - 1
    split = turned_about(split, "dp", 1, dp, dim)
    return turned_about(split, "seq", width, cubes, dim + 1).reshape(values.shape)


def near_gather(values, axis, unit, count):
    values = values[None]
    for bit in bits_of(count):
        values = jnp.concatenate([values, swap(values, axis, bit * unit)], 0)
    return values


def near_sum(values, axis, unit, count, waited=()):
    for bit in reversed(bits_of(count)):
        sent = values[bit:].astype(LOW)
        sent = swap(tie(sent, *waited) if waited else sent, axis, bit * unit)
        values = values[:bit].astype(FULL) + sent.astype(FULL)
    return values[0]


def cube_turn(values, width):
    seq = lax.axis_size("seq")
    groups = [list(range(first, first + width)) for first in range(0, seq, width)]
    return lax.all_to_all(values, "seq", 0, 0, axis_index_groups=groups, tiled=True)


def gather_all(values):
    count = lax.axis_size("dp") * lax.axis_size("seq")
    rows = jnp.broadcast_to(values[None], (count,) + values.shape)
    return lax.all_to_all(rows, ("dp", "seq"), 0, 0, tiled=True)


def sum_all(values):
    return jnp.sum(lax.all_to_all(values, ("dp", "seq"), 0, 0, tiled=True), axis=0)


def column_parts(columns, count):
    tiles = columns // 128
    edges = [128 * ((tiles * part) // count) for part in range(count + 1)]
    edges[-1] = columns
    return list(zip(edges[:-1], edges[1:]))


def cube_orders(width, parts):
    places = list(range(width.bit_length() - 1))
    if parts == 2 and len(places) > 2:
        return [places[1:] + places[:1], places[2:] + places[:2]]
    if parts == 3:
        return [places[start:] + places[:start] for start in range(len(places))] or [[]]
    return ([places[::-1], places[-1:] + places[:-1]] if len(places) > 2 else [places[::-1]])[:parts]


def cube_open(values, width, parts):
    rows, columns = values.shape
    orders = cube_orders(width, parts)
    cut = column_parts(columns, len(orders))
    return [values[:, low:high].reshape([1] * len(orders[0]) + [rows, high - low]) for low, high in cut]


def cube_step(blocks, width, parts, phase):
    orders = cube_orders(width, parts)
    depth = len(orders[0])
    return [
        grow(block, "seq", 1 << order[phase], depth - 1 - order[phase])
        for order, block in zip(orders, blocks)
    ]


def cube_close(blocks):
    return jnp.concatenate([block.reshape(-1, block.shape[-1]) for block in blocks], 1)


def cube_gather(values, width, parts):
    lead, (rows, columns) = values.shape[:-2], values.shape[-2:]
    orders = cube_orders(width, parts)
    depth = len(orders[0])
    done = []
    for order, (low, high) in zip(orders, column_parts(columns, len(orders))):
        block = values[..., low:high].reshape([1] * depth + list(values.shape[:-1]) + [high - low])
        for place in order:
            block = grow(block, "seq", 1 << place, depth - 1 - place)
        block = jnp.moveaxis(block.reshape((width,) + lead + (rows, high - low)), 0, -3)
        done.append(block.reshape(lead + (width * rows, high - low)))
    return jnp.concatenate(done, -1)


def cube_sum(values, width):
    blocks = values.astype(LOW).reshape((width, values.shape[0] // width) + values.shape[1:])
    return jnp.sum(cube_turn(blocks, width).astype(FULL), axis=0)


def cube_sum_by_axes(left, right, dot, width, middle=(), last=()):
    rows = left.shape[0]
    orders = cube_orders(width, 2)
    depth = len(orders[0])
    done = []
    for order, part in zip(orders, right):
        block = dot(left, part)
        columns = block.shape[1]
        block = block.reshape([2] * depth + [rows // width, columns])
        for step, place in enumerate(reversed(order)):
            waited = () if step == 0 else last if step == depth - 1 else middle
            block = halve(block, "seq", 1 << place, depth - 1 - place, waited)
        done.append(block.reshape(rows // width, columns))
    return jnp.concatenate(done, 1)


def fiber_gather_seq(values, width):
    values = values[None]
    for bit in bits_of(lax.axis_size("seq") // width):
        values = grow(values, "seq", bit * width, 0)
    return values


def chip_gather(values):
    for bit in bits_of(lax.axis_size("dp")):
        values = grow(values, "dp", bit, 0)
    return values


def chip_sum(values):
    rest = values.shape[1:]
    for bit in reversed(bits_of(lax.axis_size("dp"))):
        values = halve(values.reshape((2, -1) + rest), "dp", bit, 0)[0]
    return values


def far_sum(values, width, waited=(), later=()):
    rest = values.shape[1:]
    for bit in reversed(bits_of(lax.axis_size("seq") // width)):
        values = halve(values.reshape((2, -1) + rest), "seq", bit * width, 0, waited, later)[0]
    return values.reshape(rest)


CHUNK = 128
MICRO = 1 << 30
SPAN = 8
RIM = 16


def split(values):
    high = values.astype(LOW)
    return (high, (values - high.astype(FULL)).astype(LOW))


def mul(left, right):
    return jnp.dot(
        jnp.concatenate([left[0], left[1], left[0]], 1),
        jnp.concatenate([right[0], right[0], right[1]], 0),
        preferred_element_type=FULL,
    )


def mul_t(left, right):
    return lax.dot_general(
        jnp.concatenate([left[0], left[1], left[0]], 1),
        jnp.concatenate([right[0], right[0], right[1]], 1),
        (((1,), (1,)), ((), ())),
        preferred_element_type=FULL,
    )


def grid_index(dim):
    return lax.broadcasted_iota(jnp.int32, (CHUNK, CHUNK), dim)


def row_sum(values):
    return jnp.sum(values, axis=1, keepdims=True)


def here_rows(chunk):
    return pl.ds(pl.multiple_of(chunk * CHUNK + RIM, SPAN), CHUNK)


def conv_part(mix_ref, taps_ref, cols, chunk, low):
    start = pl.multiple_of(chunk * CHUNK + RIM - SPAN, SPAN)
    rows = mix_ref[pl.ds(start, CHUNK + SPAN), low : low + HEAD].astype(LOW).astype(FULL)
    total = jnp.zeros((CHUNK, HEAD), FULL)
    terms = []
    for tap in range(CONV):
        back = CONV - 1 - tap
        moved = rows if back == 0 else pltpu.roll(rows, back, 0)
        term = moved[SPAN:] * cols[:, tap : tap + 1]
        terms.append(term)
        total = total + taps_ref[tap : tap + 1, low : low + HEAD] * term
    return (total, terms)


def unit_part(values):
    scale = lax.rsqrt(row_sum(values * values) + EPS)
    return (values * scale, scale)


def prep_kernel(heads, deep, mix_ref, taps_ref, cols_ref, seg_ref, *outs):
    q_ref, k_ref, uk_ref, uv_ref, inv_ref, att_ref, map_ref, add_ref, far_ref, end_ref = outs
    mine = heads * HEAD
    chunks = seg_ref.shape[0]
    group = 2 if chunks % 2 == 0 else 1
    i_at, j_at = grid_index(0), grid_index(1)
    apart = i_at ^ j_at
    eye = (i_at == j_at).astype(FULL)

    def some(step, carry):
        work = []
        for offset in range(group):
            chunk = step * group + offset
            cols = cols_ref[pl.ds(pl.multiple_of(chunk * CHUNK, CHUNK), CHUNK), :]
            same = cols[:, 4:5] == seg_ref[chunk]
            lower = (same & (j_at < i_at)).astype(FULL)
            inclusive = (same & (j_at <= i_at)).astype(FULL)
            carried, ending = cols[:, 5:6], cols[:, 6:7]
            for head in range(heads):
                at = chunk * heads + head
                parts = [
                    jax.nn.silu(
                        conv_part(mix_ref, taps_ref, cols, chunk, part * mine + head * HEAD)[0]
                    )
                    for part in range(3)
                ]
                query, key = unit_part(parts[0])[0], unit_part(parts[1])[0]
                last = mix_ref[here_rows(chunk), 4 * mine : 4 * mine + HEAD]
                weight = jax.nn.sigmoid(last[:, head : head + 1])
                q_ref[at] = query
                k_ref[at] = key
                key_s, query_s = split(key), split(query)
                both = tuple(jnp.concatenate([a, b], 0) for a, b in zip(key_s, query_s))
                grams = mul_t(both, key_s)
                att_ref[at] = grams[CHUNK:] * inclusive
                below = weight * grams[:CHUNK] * lower
                work.append([at, key, parts[2], weight, carried, ending, below])
        inverses = [eye - jnp.where(apart == 1, item[6], 0.0) for item in work]
        level = 1
        while (1 << level) < CHUNK:
            next_inverses = []
            for item, inverse in zip(work, inverses):
                inverse_s = split(inverse)
                block = split(jnp.where((apart >> level) == 1, item[6], 0.0))
                inner = split(mul(inverse_s, block))
                next_inverses.append(inverse - mul(inner, inverse_s))
            inverses = next_inverses
            level += 1
        for item, inverse in zip(work, inverses):
            at, key, value, weight, carried, ending, below = item
            inv_ref[at] = inverse
            right = jnp.concatenate([(weight * carried) * key, weight * value], 1)
            solved = mul(split(inverse), split(right))
            uk_ref[at] = solved[:, :HEAD]
            uv_ref[at] = solved[:, HEAD:]
            turned = mul(split((key * ending).T), split(solved))
            map_ref[at] = carried[CHUNK - 1 :] * eye - turned[:, :HEAD]
            add_ref[at] = turned[:, HEAD:]
        return carry

    lax.fori_loop(0, chunks // group, some, 0)

    end_ref[...] = jnp.zeros_like(end_ref)
    for head in range(heads):
        far_ref[head] = eye

    def chain(chunk, carry):
        for head in range(heads):
            at = chunk * heads + head
            step = split(map_ref[at])
            end_ref[head] = mul(step, split(end_ref[head])) + add_ref[at]
            if deep:
                far_ref[head] = mul(step, split(far_ref[head]))
        return carry

    lax.fori_loop(0, chunks, chain, 0)


def run_kernel(heads, mix_ref, cols_ref, gain_ref, q_ref, uk_ref, uv_ref, att_ref, map_ref, add_ref, state_ref, *outs):
    p_ref, delta_ref, out_ref, scaled_ref, now_ref = outs
    mine = heads * HEAD
    chunks = p_ref.shape[0] // heads
    now_ref[...] = state_ref[...]

    def one(chunk, carry):
        start = pl.multiple_of(chunk * CHUNK, CHUNK)
        carried = cols_ref[pl.ds(start, CHUNK), :][:, 5:6]
        for head in range(heads):
            at = chunk * heads + head
            state = now_ref[head]
            p_ref[at] = state
            state_s = split(state)
            now_ref[head] = mul(split(map_ref[at]), state_s) + add_ref[at]
            both = split(jnp.concatenate([uk_ref[at], q_ref[at]], 0))
            seen = mul(both, state_s)
            delta = uv_ref[at] - seen[:CHUNK]
            delta_ref[at] = delta
            output = carried * seen[CHUNK:] + mul(split(att_ref[at]), split(delta))
            out_ref[at] = output
            low = 3 * mine + head * HEAD
            gate = mix_ref[here_rows(chunk), low : low + HEAD]
            scale = lax.rsqrt(row_sum(output * output) / HEAD + HEAD_EPS)
            gain = gain_ref[:, head * HEAD : (head + 1) * HEAD]
            scaled = output * scale * gain * jax.nn.silu(gate)
            scaled_ref[pl.ds(start, CHUNK), head * HEAD : (head + 1) * HEAD] = scaled.astype(LOW)
        return carry

    lax.fori_loop(0, chunks, one, 0)


def silu_slope(values):
    gate = jax.nn.sigmoid(values)
    return gate * (1.0 + values * (1.0 - gate))


def back_kernel(heads, mix_ref, cols_ref, gain_ref, q_ref, uk_ref, att_ref, map_ref, out_ref, grad_ref, *outs):
    dout_ref, first_ref, term_ref, dgate_ref, end_ref = outs
    mine = heads * HEAD
    chunks = out_ref.shape[0] // heads
    end_ref[...] = jnp.zeros_like(end_ref)

    def one(step, carry):
        chunk = chunks - 1 - step
        start = pl.multiple_of(chunk * CHUNK, CHUNK)
        carried = cols_ref[pl.ds(start, CHUNK), :][:, 5:6]
        for head in range(heads):
            at = chunk * heads + head
            here = slice(head * HEAD, (head + 1) * HEAD)
            low = 3 * mine + head * HEAD
            gate = mix_ref[here_rows(chunk), low : low + HEAD]
            output = out_ref[at]
            grad = grad_ref[pl.ds(start, CHUNK), here].astype(FULL)
            gain = gain_ref[:, here]
            scale = lax.rsqrt(row_sum(output * output) / HEAD + HEAD_EPS)
            unit = output * scale
            opened = jax.nn.silu(gate)
            dgate_ref[pl.ds(start, CHUNK), here] = (grad * unit * gain * silu_slope(gate)).astype(LOW)
            inner = grad * gain * opened
            dout = scale * (inner - unit * (row_sum(inner * unit) / HEAD))
            dout_ref[at] = dout
            first = mul(split(att_ref[at].T), split(dout))
            first_ref[at] = first
            left = split(jnp.concatenate([q_ref[at].T, uk_ref[at].T], 1))
            term = mul(left, split(jnp.concatenate([carried * dout, -first], 0)))
            term_ref[at] = term
            end_ref[head] = mul(split(map_ref[at].T), split(end_ref[head])) + term
        return carry

    lax.fori_loop(0, chunks, one, 0)


def pull_kernel(heads, mix_ref, taps_ref, cols_ref, seg_ref, *rest):
    (q_ref, k_ref, inv_ref, att_ref, map_ref, p_ref, delta_ref) = rest[:7]
    (dout_ref, first_ref, term_ref, dgate_ref, leave_ref) = rest[7:12]
    gmix_ref, tail_ref, edge_ref, dtaps_ref, now_ref, next_ref = rest[12:]
    gmix_ref[:RIM] = jnp.zeros((RIM, gmix_ref.shape[1]), LOW)
    mine = heads * HEAD
    chunks = seg_ref.shape[0]
    i_at, j_at = grid_index(0), grid_index(1)
    now_ref[...] = leave_ref[...]
    next_ref[...] = jnp.zeros_like(next_ref)
    dtaps_ref[...] = jnp.zeros_like(dtaps_ref)

    def one(step, carry):
        chunk = chunks - 1 - step
        start = pl.multiple_of(chunk * CHUNK, CHUNK)
        cols_far = cols_ref[pl.ds(start, CHUNK + SPAN), :]
        cols = cols_far[:CHUNK]
        same = cols[:, 4:5] == seg_ref[chunk]
        lower = (same & (j_at < i_at)).astype(FULL)
        inclusive = (same & (j_at <= i_at)).astype(FULL)
        carried, ending = cols[:, 5:6], cols[:, 6:7]
        last = mix_ref[here_rows(chunk), 4 * mine : 4 * mine + HEAD]
        dlast = jnp.zeros((CHUNK, HEAD), FULL)
        for head in range(heads):
            at = chunk * heads + head
            lows = [part * mine + head * HEAD for part in range(3)]
            mixed = [conv_part(mix_ref, taps_ref, cols, chunk, low) for low in lows]
            query, query_scale = unit_part(jax.nn.silu(mixed[0][0]))
            key, key_scale = unit_part(jax.nn.silu(mixed[1][0]))
            value = jax.nn.silu(mixed[2][0])
            weight = jax.nn.sigmoid(last[:, head : head + 1])
            key_s = split(key)
            leave = now_ref[head]
            leave_s = split(leave)
            now_ref[head] = mul(split(map_ref[at].T), leave_s) + term_ref[at]
            ddelta = first_ref[at] + mul(split(key * ending), leave_s)
            solved = mul(split(inv_ref[at].T), split(ddelta))
            delta_s = split(delta_ref[at])
            dout = dout_ref[at]
            ends = split(jnp.concatenate([solved, dout], 0))
            by_state = mul_t(ends, split(p_ref[at]))
            by_delta = mul_t(ends, delta_s)
            dright = -by_state[:CHUNK]
            dsystem = -by_delta[:CHUNK] * lower
            datt = by_delta[CHUNK:] * inclusive
            dquery = carried * by_state[CHUNK:] + mul(split(datt), key_s)
            gram = mul_t(key_s, key_s)
            dgram = weight * dsystem
            left = split(jnp.concatenate([datt.T, dgram + dgram.T], 1))
            right = tuple(jnp.concatenate([a, b], 0) for a, b in zip(split(query), key_s))
            dkey = mul(left, right) + (weight * carried) * dright
            dkey = dkey + ending * mul_t(delta_s, leave_s)
            dvalue = weight * solved
            dweight = row_sum(solved * value + carried * dright * key + dsystem * gram)
            dlogit = dweight * weight * (1.0 - weight)
            dlast = jnp.where(j_at == head, dlogit, dlast)
            dactive = [
                query_scale * (dquery - query * row_sum(dquery * query)),
                key_scale * (dkey - key * row_sum(dkey * key)),
                dvalue,
            ]
            for part, low in enumerate(lows):
                total, terms = mixed[part]
                dtotal = dactive[part] * silu_slope(total)
                here = slice(low, low + HEAD)
                far = jnp.concatenate([dtotal, next_ref[:, here]], 0)
                near = jnp.concatenate([jnp.zeros((SPAN, HEAD), FULL), dtotal[:SPAN]], 0)
                next_ref[:, here] = dtotal[:SPAN]
                dproj = jnp.zeros((CHUNK, HEAD), FULL)
                edge = jnp.zeros((SPAN, HEAD), FULL)
                zero = jnp.zeros((SPAN, 1), FULL)
                for tap in range(CONV):
                    back = CONV - 1 - tap
                    tap_row = taps_ref[tap : tap + 1, here]
                    dtaps_ref[tap : tap + 1, here] += jnp.sum(dtotal * terms[tap], axis=0, keepdims=True)
                    spread = far * cols_far[:, tap : tap + 1]
                    near_mask = jnp.concatenate([zero, cols[:SPAN, tap : tap + 1]], 0)
                    close = near * near_mask
                    if back > 0:
                        spread = pltpu.roll(spread, CHUNK + SPAN - back, 0)
                        close = pltpu.roll(close, 2 * SPAN - back, 0)
                        edge = edge + tap_row * close[:SPAN]
                    dproj = dproj + tap_row * spread[:CHUNK]
                gmix_ref[here_rows(chunk), here] = dproj.astype(LOW)
                edge_ref[:, here] = edge

                @pl.when(step == 0)
                def _():
                    tail_ref[:, here] = dproj[CHUNK - SPAN :]

        gmix_ref[here_rows(chunk), 3 * mine : 4 * mine] = dgate_ref[pl.ds(start, CHUNK), :]
        gmix_ref[here_rows(chunk), 4 * mine : 4 * mine + HEAD] = dlast.astype(LOW)
        return carry

    lax.fori_loop(0, chunks, one, 0)
    gap = jnp.zeros((RIM - SPAN, 3 * mine), FULL)
    gmix_ref[:RIM, : 3 * mine] = jnp.concatenate([gap, edge_ref[...]], 0).astype(LOW)


def on_chip(body, shapes, scratch, flops, waited, *operands):
    whole = pl.BlockSpec(memory_space=pltpu.VMEM)
    anywhere = pl.BlockSpec(memory_space=pl.ANY)
    used, spare = len(operands), len(waited)
    return pl.pallas_call(
        lambda *refs: body(*refs[:used], *refs[used + spare :]),
        out_shape=shapes,
        in_specs=[whole] * used + [anywhere] * spare,
        out_specs=[whole] * len(shapes),
        scratch_shapes=list(scratch),
        compiler_params=pltpu.CompilerParams(vmem_limit_bytes=56 * 1024 * 1024),
        cost_estimate=pl.CostEstimate(flops=flops, bytes_accessed=20 * 1024 * 1024, transcendentals=0),
    )(*operands, *waited)


def squares(*counts):
    return tuple(jax.ShapeDtypeStruct((count, HEAD, HEAD), FULL) for count in counts)


def delta_prep(heads, deep, mix, taps, cols, segs, waited):
    each = segs.shape[0] * heads
    shapes = squares(*[each] * 8, heads, heads)
    body = functools.partial(prep_kernel, heads, deep)
    return on_chip(body, shapes, (), 30 * MICRO, waited, mix, taps, cols, segs)


def delta_run(heads, mix, cols, gain, prepared, state, waited):
    q, k, uk, uv, inv, att, step, add = prepared
    each = q.shape[0]
    count = each // heads * CHUNK
    shapes = squares(each, each, each) + (jax.ShapeDtypeStruct((count, heads * HEAD), LOW),)
    body = functools.partial(run_kernel, heads)
    scratch = [pltpu.VMEM((heads, HEAD, HEAD), FULL)]
    flops = 11 * MICRO
    return on_chip(
        body, shapes, scratch, flops, waited, mix, cols, gain, q, uk, uv, att, step, add, state
    )


def delta_back(heads, mix, cols, gain, prepared, output, grad, waited):
    q, k, uk, uv, inv, att, step, add = prepared
    each = q.shape[0]
    count = each // heads * CHUNK
    mine = heads * HEAD
    shapes = squares(each, each, each) + (
        jax.ShapeDtypeStruct((count, mine), LOW),
    ) + squares(heads)
    body = functools.partial(back_kernel, heads)
    flops = 12 * MICRO
    return on_chip(
        body, shapes, (), flops, waited, mix, cols, gain, q, uk, att, step, output, grad
    )


def delta_pull(heads, mix, taps, cols, segs, prepared, states, delta, backs, leaving, waited):
    q, k, uk, uv, inv, att, step, add = prepared
    dout, first, term, dgate = backs
    mine = heads * HEAD
    shapes = (
        jax.ShapeDtypeStruct(mix.shape, LOW),
        jax.ShapeDtypeStruct((SPAN, 3 * mine), FULL),
        jax.ShapeDtypeStruct((SPAN, 3 * mine), FULL),
        jax.ShapeDtypeStruct((SPAN, 3 * mine), FULL),
    )
    body = functools.partial(pull_kernel, heads)
    scratch = [pltpu.VMEM((heads, HEAD, HEAD), FULL), pltpu.VMEM((SPAN, 3 * mine), FULL)]
    flops = 30 * MICRO
    return on_chip(
        body, shapes, scratch, flops, waited, mix, taps, cols, segs, q, k, inv, att, step, states, delta, dout, first, term, dgate, leaving
    )


def swiglu(gate_two, up_two):
    return jax.nn.silu(gate_two) * up_two


def local(
    block_input,
    segments,
    mix_gain,
    w_project,
    conv_taps,
    w_beta,
    w_gate,
    head_gain,
    w_output,
    ffn_gain,
    w_hidden_gate,
    w_hidden_up,
    w_hidden_down,
    cotangent,
):
    dp, seq = lax.axis_size("dp"), lax.axis_size("seq")
    width = min(WIDTH, seq & -seq)
    cubes = seq // width
    everyone = dp * seq
    fiber = dp * cubes
    both = ("dp", "seq")
    row_at, chip_at = lax.axis_index("dp"), lax.axis_index("seq")
    me = chip_at % width
    cube_at = chip_at // width
    heads = H // width
    mine = heads * HEAD
    rows = w_project.shape[0]
    tokens = block_input.shape[1]
    count = tokens * width
    units = w_hidden_down.shape[0]
    hidden_mine = fiber * units

    taps_each = conv_taps.shape[1]
    packed = jnp.concatenate(
        [
            mix_gain.astype(LOW),
            head_gain.astype(LOW),
            ffn_gain.astype(LOW),
            conv_taps.astype(LOW).reshape(-1),
            segments[0].astype(LOW),
        ]
    )
    mixer_pad = -(mine * 4 + heads) % 128
    mixer_low = jnp.concatenate(
        [
            jnp.swapaxes(w_project.reshape(rows, 3, width, mine), 1, 2).reshape(rows, width, 3 * mine),
            w_gate.reshape(rows, width, mine),
            w_beta.reshape(rows, width, heads),
            jnp.zeros((rows, width, mixer_pad), FULL),
        ],
        -1,
    ).astype(LOW)
    mixer_turned = cube_turn(jnp.swapaxes(mixer_low, 0, 1), width)
    small = gather_all(packed)
    gain_one = small[:, :rows].reshape(D).astype(FULL)
    gain_head = small[:, rows : 2 * rows].reshape(D).astype(FULL)
    gain_two = small[:, 2 * rows : 3 * rows].reshape(D).astype(FULL)
    taps_full = small[:, 3 * rows : 3 * rows + CONV * taps_each].reshape(everyone, CONV, taps_each)
    taps_full = jnp.swapaxes(taps_full, 0, 1).reshape(CONV, 3, width, mine).astype(FULL)
    taps_mine = lax.dynamic_index_in_dim(taps_full, me, 2, False).reshape(CONV, 3 * mine)
    gain_mine = lax.dynamic_index_in_dim(gain_head.reshape(width, heads, HEAD), me, 0, False)
    seg_all = small[:, 3 * rows + CONV * taps_each :].astype(jnp.int32).reshape(dp, seq * tokens)
    seg_row = lax.dynamic_index_in_dim(seg_all, row_at, 0, False)
    ext_seg = lax.dynamic_slice_in_dim(
        jnp.concatenate([jnp.zeros((CONV - 1,), jnp.int32), seg_row]),
        cube_at * count,
        count + CONV - 1,
    )
    seg_mine = ext_seg[CONV - 1 :]
    tokens_in = jnp.concatenate([fiber_order(block_input, width), cotangent], 0)
    pair = cube_gather(tokens_in, width, 2)
    x_cube, g_out = pair[0], pair[1]
    ahead = [(i, i + width) for i in range(seq - width)]
    behind = [(i + width, i) for i in range(seq - width)]
    rim = lax.ppermute(fiber_order(x_cube[count - RIM :], width), "seq", ahead)
    x_more = jnp.concatenate([fiber_order(rim, width), x_cube], 0)
    mixer_far = near_gather(mixer_turned, "seq", width, cubes)
    mixer_w = near_gather(mixer_far, "dp", 1, dp).reshape(D, -1)

    hgate_late, hup_late = hint((w_hidden_gate, w_hidden_up), mixer_turned)

    def by_units(weight):
        split = weight.astype(LOW).reshape(rows, dp, cubes, width, units)
        return jnp.transpose(split, (3, 0, 1, 2, 4)).reshape(width, rows, hidden_mine)

    ffn_low = jnp.concatenate([by_units(hgate_late), by_units(hup_late)], -1)
    ffn_turned = cube_turn(ffn_low, width)
    ffn_far = near_gather(hint(ffn_turned, mixer_far), "seq", width, cubes)

    residual = block_input[0].astype(FULL)
    normed_own, mix_pull = jax.vjp(lambda v: rms_scale(v, gain_one), residual)
    normed = rms_scale(x_more.astype(FULL), fiber_order(gain_one, width)).astype(LOW)
    mixed_in = dot_low(normed, mixer_w)
    out_low, down_low, mixed_in = lax.optimization_barrier(
        (w_output.astype(LOW), w_hidden_down.astype(LOW), mixed_in)
    )
    out_far = near_gather(out_low, "seq", width, cubes)
    out_spread = jnp.broadcast_to(out_far[None], (width,) + out_far.shape)
    out_near = cube_turn(out_spread, width).reshape(D // dp, D)
    chunks = count // CHUNK
    seg_chunks = seg_mine.reshape(chunks, CHUNK)
    before = jnp.concatenate([ext_seg[CONV - 2 : CONV - 1], seg_chunks[:-1, -1]], 0)
    columns = [ext_seg[tap : tap + count] == seg_mine for tap in range(CONV)]
    columns.append(seg_mine)
    columns.append((seg_chunks == before[:, None]).reshape(count))
    columns.append((seg_chunks == seg_chunks[:, -1:]).reshape(count))
    columns.append(jnp.zeros((count,), FULL))
    cols = jnp.stack([column.astype(FULL) for column in columns], 1)
    cols = jnp.pad(cols, ((0, SPAN), (0, 0)))
    segs = seg_chunks.astype(FULL)[:, None, :]
    gain_row = gain_mine.reshape(1, mine)
    prepared = delta_prep(heads, cubes > 2, mixed_in, taps_mine, cols, segs, ())
    far, end = prepared[8:]
    prepared = prepared[:8]
    state_in = jnp.zeros((heads, HEAD, HEAD), FULL)
    for hop in range(cubes - 1):
        out = end
        if hop > 0:
            out = end + jnp.einsum("hij,hjk->hik", far, state_in, precision=HIGH)
        state_in = lax.ppermute(out, "seq", ahead)
    states, delta, recalled, scaled = delta_run(
        heads, mixed_in, cols, gain_row, prepared, state_in, ()
    )
    ffn_w = near_gather(ffn_far, "dp", 1, dp).reshape(D, 2 * hidden_mine)
    out_parts = [out_near]
    for bit in bits_of(dp):
        out_parts = out_parts + [swap(part, "dp", bit) for part in out_parts]
    scaled_own = jnp.swapaxes(cube_turn(scaled.reshape(width, tokens, mine), width), 0, 1)
    down_w = chip_gather(fiber_gather_seq(down_low, width)).reshape(hidden_mine, D)
    scaled_own = fiber_order(scaled_own.reshape(tokens, D), width)
    scaled_own = jnp.swapaxes(scaled_own.reshape(tokens, dp, cubes, width, rows), 2, 3)
    scaled_own = scaled_own.reshape(tokens, dp, D // dp)
    middle = residual
    for at, part in enumerate(out_parts):
        middle = middle + dot_low(scaled_own[:, at], part)

    normed_two_f, ffn_pull = jax.vjp(lambda v: rms_scale(v, gain_two), middle)
    normed_two = cube_gather(fiber_order(normed_two_f.astype(LOW), width), width, 3)
    both_two = dot_low(normed_two, ffn_w)
    gate_two, up_two = both_two[:, :hidden_mine], both_two[:, hidden_mine:]
    hidden_f, glu_pull = jax.vjp(swiglu, gate_two, up_two)
    hidden = hidden_f.astype(LOW)
    grad_hidden = dot_right_t(g_out, down_w)
    grad_gate_two, grad_up_two = glu_pull(grad_hidden)
    grad_both = jnp.concatenate([grad_gate_two.astype(LOW), grad_up_two.astype(LOW)], 1)
    pulled = dot_right_t(grad_both, ffn_w).astype(LOW)
    grad_normed_two = fiber_order(cube_sum(pulled, width), width)
    grad_down = chip_sum(dot_left_t(hidden, g_out).reshape(fiber, units, D))
    grad_ffn = dot_left_t(normed_two, grad_both).reshape(dp, cubes, width, rows, -1)
    grad_ffn = near_sum(grad_ffn, "dp", 1, dp)
    grad_normed_two, grad_ffn, grad_down = lax.optimization_barrier(
        (grad_normed_two, grad_ffn, grad_down)
    )
    (grad_middle,) = ffn_pull(grad_normed_two)
    grad_middle = grad_middle + cotangent[0].astype(FULL)
    grad_branch = grad_middle.astype(LOW)
    grad_scaled_own = jnp.stack([dot_right_t(grad_branch, part).astype(LOW) for part in out_parts], 1)
    grad_scaled_own = jnp.swapaxes(grad_scaled_own.reshape(tokens, dp, width, cubes, rows), 2, 3)
    grad_scaled_own = fiber_order(grad_scaled_own.reshape(tokens, D), width)

    grad_scaled = cube_turn(
        jnp.swapaxes(grad_scaled_own.reshape(tokens, width, mine), 0, 1), width
    ).reshape(count, mine)
    owners = []
    for row in range(dp):
        for chip in range(seq):
            block = (chip % width) * fiber + row * cubes + chip // width
            owners.append((row * seq + chip, block))
    groups = [list(range(first, first + width)) for first in range(0, seq, width)]
    branch_cube = cube_turn(jnp.broadcast_to(tie(grad_branch, grad_scaled)[None], (width, tokens, D)), width)
    branch_cube = branch_cube.reshape(count, D)
    half = D // len(cube_orders(width, 2))
    down_parts = [down_w[:, at : at + half] for at in range(0, D, half)]
    backs = delta_back(
        heads, mixed_in, cols, gain_row, prepared, recalled, grad_scaled, ()
    )
    end_back = backs[4]
    leaving = jnp.zeros((heads, HEAD, HEAD), FULL)
    for hop in range(cubes - 1):
        out = end_back
        if hop > 0:
            out = end_back + jnp.einsum("hji,hjk->hik", far, leaving, precision=HIGH)
        leaving = lax.ppermute(out, "seq", behind)
    grad_ffn = near_sum(grad_ffn, "seq", width, cubes, (leaving,)).astype(LOW)
    grad_mixed, tail, edge, grad_taps = delta_pull(
        heads, mixed_in, taps_mine, cols, segs, prepared, states, delta, backs[:4], leaving,
        (),
    )
    result = middle + cube_sum_by_axes(tie(hidden, edge), down_parts, dot_low, width)
    block_output = result.astype(LOW)[None]
    grad_mixed = tie(grad_mixed, branch_cube)
    grad_mixer = dot_left_t(normed, grad_mixed).reshape(dp, cubes, width, rows, -1)
    grad_mixer = near_sum(grad_mixer, "dp", 1, dp)
    from_next = lax.ppermute(edge.astype(LOW), "seq", behind).astype(FULL)
    grad_fixed = lax.dynamic_update_slice(
        grad_mixed[RIM:], (tail + from_next).astype(LOW), (count - SPAN, 0)
    )
    grad_taps = grad_taps[:CONV]
    grad_fixed = tie(grad_fixed, grad_mixer)
    mixer_parts = [mixer_w[at : at + half] for at in range(0, D, half)]
    grad_oproj = chip_sum(dot_left_t(scaled, branch_cube).reshape(fiber, rows, D))
    grad_oproj = far_sum(grad_oproj, width, (grad_ffn,))
    grad_mixer = near_sum(grad_mixer, "seq", width, cubes, (grad_ffn, grad_oproj)).astype(LOW)
    mixer_far_sum = grad_mixer
    grad_normed = cube_sum_by_axes(grad_fixed, mixer_parts, dot_right_t, width)
    grad_normed = fiber_order(grad_normed, width)
    grad_oproj = lax.ppermute(grad_oproj.astype(LOW), both, owners).astype(FULL)
    grad_ffn = cube_turn(tie(grad_ffn, grad_normed), width)
    taps_wide = lax.dynamic_update_index_in_dim(
        jnp.zeros((CONV, 3, width, mine), FULL), grad_taps.reshape(CONV, 3, mine), me, 2
    ).reshape(CONV, everyone, taps_each)
    taps_wide = jnp.swapaxes(taps_wide, 0, 1).reshape(everyone, CONV * taps_each)
    taps_own = sum_all(taps_wide)
    grad_mixer = cube_turn(tie(grad_mixer, grad_ffn, taps_own, block_output), width).astype(FULL)
    grad_ffn = grad_ffn.astype(FULL)

    def by_rows(grad):
        split = grad.reshape(width, rows, dp, cubes, units)
        return jnp.transpose(split, (1, 2, 3, 0, 4)).reshape(rows, -1)

    grad_hgate, grad_hup = by_rows(grad_ffn[..., :hidden_mine]), by_rows(grad_ffn[..., hidden_mine:])
    grad_mixer = jnp.swapaxes(grad_mixer, 0, 1)
    grad_wproj = jnp.swapaxes(grad_mixer[..., : 3 * mine].reshape(rows, width, 3, mine), 1, 2)
    grad_wproj = grad_wproj.reshape(rows, 3 * D)
    grad_wgate = grad_mixer[..., 3 * mine : 4 * mine].reshape(rows, D)
    grad_wbeta = grad_mixer[..., 4 * mine : 4 * mine + heads].reshape(rows, H)
    grad_down = far_sum(grad_down, width, (mixer_far_sum,), (grad_hgate, grad_hup))
    (grad_tokens,) = mix_pull(grad_normed)
    grad_input = (grad_tokens + grad_middle)[None]

    def gain_grad(gain, *pairs):
        terms = [row_sum(weight.astype(LOW).astype(FULL) * grad) for weight, grad in pairs]
        return sum(terms)[:, 0] / gain.astype(LOW).astype(FULL)

    grad_mgain = gain_grad(mix_gain, (w_project, grad_wproj), (w_gate, grad_wgate), (w_beta, grad_wbeta))
    grad_hgain = gain_grad(head_gain, (w_output, grad_oproj))
    grad_fgain = gain_grad(ffn_gain, (w_hidden_gate, grad_hgate), (w_hidden_up, grad_hup))
    return (
        block_output,
        grad_input,
        grad_mgain,
        grad_wproj,
        taps_own.reshape(CONV, taps_each),
        grad_wbeta,
        grad_wgate,
        grad_hgain,
        grad_oproj,
        grad_fgain,
        grad_hgate,
        grad_hup,
        grad_down,
    )


def solution(mesh):
    tokens = P("dp", "seq", None)
    vector = P(("dp", "seq"))
    matrix = P(("dp", "seq"), None)
    taps = P(None, ("dp", "seq"))
    in_specs = (tokens, P("dp", "seq"), vector, matrix, taps, matrix, matrix, vector, matrix)
    in_specs = in_specs + (vector, matrix, matrix, matrix, tokens)
    out_specs = (tokens, tokens, vector, matrix, taps, matrix, matrix, vector, matrix)
    out_specs = out_specs + (vector, matrix, matrix, matrix)
    return jax.shard_map(local, mesh=mesh, in_specs=in_specs, out_specs=out_specs, check_vma=False)
```

```python
import functools

import jax
import jax.numpy as jnp
from jax import lax
from jax.experimental import pallas as pl
from jax.experimental.pallas import tpu as pltpu
from jax.sharding import PartitionSpec as P

D = 2048
H = 16
HEAD = 128
CONV = 4
WIDTH = 8


EPS = 1e-06
HEAD_EPS = 0.01
HIGH = lax.Precision.HIGHEST
LOW = jnp.bfloat16
FULL = jnp.float32


def rms_scale(values, gain):
    return values * lax.rsqrt(jnp.mean(values * values, axis=-1, keepdims=True) + EPS) * gain


def dot_low(left, right):
    return jnp.dot(left, right, preferred_element_type=FULL)


def dot_left_t(left, right):
    return lax.dot_general(left, right, (((0,), (0,)), ((), ())), preferred_element_type=FULL)


def dot_right_t(left, right):
    return lax.dot_general(left, right, (((1,), (1,)), ((), ())), preferred_element_type=FULL)


def bits_of(count):
    return [1 << place for place in range(count.bit_length() - 1)]


def swap(values, axis, bit):
    return lax.ppermute(values, axis, [(i, i ^ bit) for i in range(lax.axis_size(axis))])


def grow(values, axis, bit, dim):
    upper = ((lax.axis_index(axis) & bit) != 0).astype(jnp.int32)
    other = swap(values, axis, bit)
    shape = values.shape[:dim] + (2,) + values.shape[dim:]
    own = lax.broadcasted_iota(jnp.int32, shape, dim) == upper
    both = jnp.where(own, jnp.expand_dims(values, dim), jnp.expand_dims(other, dim))
    return both.reshape(values.shape[:dim] + (2 * values.shape[dim],) + values.shape[dim + 1 :])


def halve(values, axis, bit, dim, waited=(), later=()):
    upper = ((lax.axis_index(axis) & bit) != 0).astype(jnp.int32)
    kept = lax.dynamic_index_in_dim(values, upper, dim, True)
    sent = lax.dynamic_index_in_dim(values, 1 - upper, dim, True)
    sent = sent.astype(LOW)
    come = swap(tie(sent, *waited) if waited else sent, axis, bit)
    return kept.astype(FULL) + (tie(come, *later) if later else come).astype(FULL)


def tie(values, *others):
    leaves, tree = jax.tree.flatten(values)
    waited = jax.tree.leaves(others)
    anywhere = pl.BlockSpec(memory_space=pl.ANY)
    passed = pl.pallas_call(
        lambda *refs: None,
        out_shape=[jax.ShapeDtypeStruct(leaf.shape, leaf.dtype) for leaf in leaves],
        in_specs=[anywhere] * (len(leaves) + len(waited)),
        out_specs=[anywhere] * len(leaves),
        input_output_aliases={at: at for at in range(len(leaves))},
        cost_estimate=pl.CostEstimate(flops=1024, bytes_accessed=1024, transcendentals=0),
    )(*leaves, *waited)
    return jax.tree.unflatten(tree, passed)


def hint(values, *others):
    return lax.optimization_barrier((values, *others))[0]


def turned_about(values, axis, unit, count, dim):
    place = lax.axis_index(axis) // unit
    shape = values.shape
    for bit in bits_of(count):
        split = values.reshape(shape[:dim] + (count // (2 * bit), 2, bit) + shape[dim + 1 :])
        flipped = jnp.flip(split, dim + 1)
        values = jnp.where((place & bit) != 0, flipped, split).reshape(shape)
    return values


def fiber_order(values, width):
    dp, cubes = lax.axis_size("dp"), lax.axis_size("seq") // width
    split = values.reshape(values.shape[:-1] + (dp, cubes, -1))
    dim = values.ndim - 1
    split = turned_about(split, "dp", 1, dp, dim)
    return turned_about(split, "seq", width, cubes, dim + 1).reshape(values.shape)


def near_gather(values, axis, unit, count):
    values = values[None]
    for bit in bits_of(count):
        values = jnp.concatenate([values, swap(values, axis, bit * unit)], 0)
    return values


def near_sum(values, axis, unit, count, waited=()):
    for bit in reversed(bits_of(count)):
        sent = values[bit:].astype(LOW)
        sent = swap(tie(sent, *waited) if waited else sent, axis, bit * unit)
        values = values[:bit].astype(FULL) + sent.astype(FULL)
    return values[0]


def cube_turn(values, width):
    seq = lax.axis_size("seq")
    groups = [list(range(first, first + width)) for first in range(0, seq, width)]
    return lax.all_to_all(values, "seq", 0, 0, axis_index_groups=groups, tiled=True)


def gather_all(values):
    count = lax.axis_size("dp") * lax.axis_size("seq")
    rows = jnp.broadcast_to(values[None], (count,) + values.shape)
    return lax.all_to_all(rows, ("dp", "seq"), 0, 0, tiled=True)


def sum_all(values):
    return jnp.sum(lax.all_to_all(values, ("dp", "seq"), 0, 0, tiled=True), axis=0)


def column_parts(columns, count):
    tiles = columns // 128
    edges = [128 * ((tiles * part) // count) for part in range(count + 1)]
    edges[-1] = columns
    return list(zip(edges[:-1], edges[1:]))


def cube_orders(width, parts):
    places = list(range(width.bit_length() - 1))
    if parts == 2 and len(places) > 2:
        return [places[1:] + places[:1], places[2:] + places[:2]]
    if parts == 3:
        return [places[start:] + places[:start] for start in range(len(places))] or [[]]
    return ([places[::-1], places[-1:] + places[:-1]] if len(places) > 2 else [places[::-1]])[:parts]


def cube_open(values, width, parts):
    rows, columns = values.shape
    orders = cube_orders(width, parts)
    cut = column_parts(columns, len(orders))
    return [values[:, low:high].reshape([1] * len(orders[0]) + [rows, high - low]) for low, high in cut]


def cube_step(blocks, width, parts, phase):
    orders = cube_orders(width, parts)
    depth = len(orders[0])
    return [
        grow(block, "seq", 1 << order[phase], depth - 1 - order[phase])
        for order, block in zip(orders, blocks)
    ]


def cube_close(blocks):
    return jnp.concatenate([block.reshape(-1, block.shape[-1]) for block in blocks], 1)


def cube_gather(values, width, parts):
    lead, (rows, columns) = values.shape[:-2], values.shape[-2:]
    orders = cube_orders(width, parts)
    depth = len(orders[0])
    done = []
    for order, (low, high) in zip(orders, column_parts(columns, len(orders))):
        block = values[..., low:high].reshape([1] * depth + list(values.shape[:-1]) + [high - low])
        for place in order:
            block = grow(block, "seq", 1 << place, depth - 1 - place)
        block = jnp.moveaxis(block.reshape((width,) + lead + (rows, high - low)), 0, -3)
        done.append(block.reshape(lead + (width * rows, high - low)))
    return jnp.concatenate(done, -1)


def cube_sum(values, width):
    blocks = values.astype(LOW).reshape((width, values.shape[0] // width) + values.shape[1:])
    return jnp.sum(cube_turn(blocks, width).astype(FULL), axis=0)


def cube_sum_by_axes(left, right, dot, width, middle=(), last=()):
    rows = left.shape[0]
    orders = cube_orders(width, 2)
    depth = len(orders[0])
    done = []
    for order, part in zip(orders, right):
        block = dot(left, part)
        columns = block.shape[1]
        block = block.reshape([2] * depth + [rows // width, columns])
        for step, place in enumerate(reversed(order)):
            waited = () if step == 0 else last if step == depth - 1 else middle
            block = halve(block, "seq", 1 << place, depth - 1 - place, waited)
        done.append(block.reshape(rows // width, columns))
    return jnp.concatenate(done, 1)


def fiber_gather_seq(values, width):
    values = values[None]
    for bit in bits_of(lax.axis_size("seq") // width):
        values = grow(values, "seq", bit * width, 0)
    return values


def chip_gather(values):
    for bit in bits_of(lax.axis_size("dp")):
        values = grow(values, "dp", bit, 0)
    return values


def chip_sum(values):
    rest = values.shape[1:]
    for bit in reversed(bits_of(lax.axis_size("dp"))):
        values = halve(values.reshape((2, -1) + rest), "dp", bit, 0)[0]
    return values


def far_sum(values, width, waited=(), later=()):
    rest = values.shape[1:]
    for bit in reversed(bits_of(lax.axis_size("seq") // width)):
        values = halve(values.reshape((2, -1) + rest), "seq", bit * width, 0, waited, later)[0]
    return values.reshape(rest)


CHUNK = 128
MICRO = 1 << 30
SPAN = 8
RIM = 16


def split(values):
    high = values.astype(LOW)
    return (high, (values - high.astype(FULL)).astype(LOW))


def mul(left, right):
    return jnp.dot(
        jnp.concatenate([left[0], left[1], left[0]], 1),
        jnp.concatenate([right[0], right[0], right[1]], 0),
        preferred_element_type=FULL,
    )


def mul_t(left, right):
    return lax.dot_general(
        jnp.concatenate([left[0], left[1], left[0]], 1),
        jnp.concatenate([right[0], right[0], right[1]], 1),
        (((1,), (1,)), ((), ())),
        preferred_element_type=FULL,
    )


def mul_once(left, right):
    return jnp.dot(left.astype(LOW), right.astype(LOW), preferred_element_type=FULL)


def mul_once_t(left, right):
    return dot_right_t(left.astype(LOW), right.astype(LOW))


def grid_index(dim):
    return lax.broadcasted_iota(jnp.int32, (CHUNK, CHUNK), dim)


def row_sum(values):
    return jnp.sum(values, axis=1, keepdims=True)


def here_rows(chunk):
    return pl.ds(pl.multiple_of(chunk * CHUNK + RIM, SPAN), CHUNK)


def conv_part(mix_ref, taps_ref, cols, chunk, low):
    start = pl.multiple_of(chunk * CHUNK + RIM - SPAN, SPAN)
    rows = mix_ref[pl.ds(start, CHUNK + SPAN), low : low + HEAD].astype(LOW).astype(FULL)
    total = jnp.zeros((CHUNK, HEAD), FULL)
    terms = []
    for tap in range(CONV):
        back = CONV - 1 - tap
        moved = rows if back == 0 else pltpu.roll(rows, back, 0)
        term = moved[SPAN:] * cols[:, tap : tap + 1]
        terms.append(term)
        total = total + taps_ref[tap : tap + 1, low : low + HEAD] * term
    return (total, terms)


def unit_part(values):
    scale = lax.rsqrt(row_sum(values * values) + EPS)
    return (values * scale, scale)


def prep_kernel(heads, deep, mix_ref, taps_ref, cols_ref, seg_ref, *outs):
    q_ref, k_ref, uk_ref, uv_ref, inv_ref, att_ref, map_ref, add_ref, far_ref, end_ref = outs
    mine = heads * HEAD
    chunks = seg_ref.shape[0]
    group = 2 if chunks % 2 == 0 else 1
    i_at, j_at = grid_index(0), grid_index(1)
    apart = i_at ^ j_at
    eye = (i_at == j_at).astype(FULL)

    def some(step, carry):
        work = []
        for offset in range(group):
            chunk = step * group + offset
            cols = cols_ref[pl.ds(pl.multiple_of(chunk * CHUNK, CHUNK), CHUNK), :]
            same = cols[:, 4:5] == seg_ref[chunk]
            lower = (same & (j_at < i_at)).astype(FULL)
            inclusive = (same & (j_at <= i_at)).astype(FULL)
            carried, ending = cols[:, 5:6], cols[:, 6:7]
            for head in range(heads):
                at = chunk * heads + head
                parts = [
                    jax.nn.silu(
                        conv_part(mix_ref, taps_ref, cols, chunk, part * mine + head * HEAD)[0]
                    )
                    for part in range(3)
                ]
                query, key = unit_part(parts[0])[0], unit_part(parts[1])[0]
                last = mix_ref[here_rows(chunk), 4 * mine : 4 * mine + HEAD]
                weight = jax.nn.sigmoid(last[:, head : head + 1])
                q_ref[at] = query
                k_ref[at] = key
                key_s, query_s = split(key), split(query)
                both = tuple(jnp.concatenate([a, b], 0) for a, b in zip(key_s, query_s))
                grams = mul_t(both, key_s)
                att_ref[at] = grams[CHUNK:] * inclusive
                below = weight * grams[:CHUNK] * lower
                work.append([at, key, parts[2], weight, carried, ending, below])
        inverses = [eye - jnp.where(apart == 1, item[6], 0.0) for item in work]
        level = 1
        while (1 << level) < CHUNK:
            next_inverses = []
            for item, inverse in zip(work, inverses):
                inverse_s = split(inverse)
                block = split(jnp.where((apart >> level) == 1, item[6], 0.0))
                inner = split(mul(inverse_s, block))
                next_inverses.append(inverse - mul(inner, inverse_s))
            inverses = next_inverses
            level += 1
        for item, inverse in zip(work, inverses):
            at, key, value, weight, carried, ending, below = item
            inv_ref[at] = inverse
            right = jnp.concatenate([(weight * carried) * key, weight * value], 1)
            solved = mul(split(inverse), split(right))
            uk_ref[at] = solved[:, :HEAD]
            uv_ref[at] = solved[:, HEAD:]
            turned = mul(split((key * ending).T), split(solved))
            map_ref[at] = carried[CHUNK - 1 :] * eye - turned[:, :HEAD]
            add_ref[at] = turned[:, HEAD:]
        return carry

    lax.fori_loop(0, chunks // group, some, 0)

    end_ref[...] = jnp.zeros_like(end_ref)
    for head in range(heads):
        far_ref[head] = eye

    def chain(chunk, carry):
        for head in range(heads):
            at = chunk * heads + head
            step = split(map_ref[at])
            end_ref[head] = mul(step, split(end_ref[head])) + add_ref[at]
            if deep:
                far_ref[head] = mul(step, split(far_ref[head]))
        return carry

    lax.fori_loop(0, chunks, chain, 0)


def run_kernel(heads, mix_ref, cols_ref, gain_ref, q_ref, uk_ref, uv_ref, att_ref, map_ref, add_ref, state_ref, *outs):
    p_ref, delta_ref, out_ref, scaled_ref, now_ref = outs
    mine = heads * HEAD
    chunks = p_ref.shape[0] // heads
    now_ref[...] = state_ref[...]

    def one(chunk, carry):
        start = pl.multiple_of(chunk * CHUNK, CHUNK)
        carried = cols_ref[pl.ds(start, CHUNK), :][:, 5:6]
        for head in range(heads):
            at = chunk * heads + head
            state = now_ref[head]
            p_ref[at] = state
            state_s = split(state)
            now_ref[head] = mul(split(map_ref[at]), state_s) + add_ref[at]
            both = split(jnp.concatenate([uk_ref[at], q_ref[at]], 0))
            seen = mul(both, state_s)
            delta = uv_ref[at] - seen[:CHUNK]
            delta_ref[at] = delta
            output = carried * seen[CHUNK:] + mul(split(att_ref[at]), split(delta))
            out_ref[at] = output
            low = 3 * mine + head * HEAD
            gate = mix_ref[here_rows(chunk), low : low + HEAD]
            scale = lax.rsqrt(row_sum(output * output) / HEAD + HEAD_EPS)
            gain = gain_ref[:, head * HEAD : (head + 1) * HEAD]
            scaled = output * scale * gain * jax.nn.silu(gate)
            scaled_ref[pl.ds(start, CHUNK), head * HEAD : (head + 1) * HEAD] = scaled.astype(LOW)
        return carry

    lax.fori_loop(0, chunks, one, 0)


def silu_slope(values):
    gate = jax.nn.sigmoid(values)
    return gate * (1.0 + values * (1.0 - gate))


def back_kernel(heads, mix_ref, cols_ref, gain_ref, q_ref, uk_ref, att_ref, map_ref, out_ref, grad_ref, *outs):
    dout_ref, first_ref, term_ref, dgate_ref, end_ref = outs
    mine = heads * HEAD
    chunks = out_ref.shape[0] // heads
    end_ref[...] = jnp.zeros_like(end_ref)

    def one(step, carry):
        chunk = chunks - 1 - step
        start = pl.multiple_of(chunk * CHUNK, CHUNK)
        carried = cols_ref[pl.ds(start, CHUNK), :][:, 5:6]
        for head in range(heads):
            at = chunk * heads + head
            here = slice(head * HEAD, (head + 1) * HEAD)
            low = 3 * mine + head * HEAD
            gate = mix_ref[here_rows(chunk), low : low + HEAD]
            output = out_ref[at]
            grad = grad_ref[pl.ds(start, CHUNK), here].astype(FULL)
            gain = gain_ref[:, here]
            scale = lax.rsqrt(row_sum(output * output) / HEAD + HEAD_EPS)
            unit = output * scale
            opened = jax.nn.silu(gate)
            dgate_ref[pl.ds(start, CHUNK), here] = (grad * unit * gain * silu_slope(gate)).astype(LOW)
            inner = grad * gain * opened
            dout = scale * (inner - unit * (row_sum(inner * unit) / HEAD))
            dout_ref[at] = dout
            first = mul(split(att_ref[at].T), split(dout))
            first_ref[at] = first
            left = split(jnp.concatenate([q_ref[at].T, uk_ref[at].T], 1))
            term = mul(left, split(jnp.concatenate([carried * dout, -first], 0)))
            term_ref[at] = term
            end_ref[head] = mul(split(map_ref[at].T), split(end_ref[head])) + term
        return carry

    lax.fori_loop(0, chunks, one, 0)


def pull_kernel(heads, mix_ref, taps_ref, cols_ref, seg_ref, *rest):
    (q_ref, k_ref, inv_ref, att_ref, map_ref, p_ref, delta_ref) = rest[:7]
    (dout_ref, first_ref, term_ref, dgate_ref, leave_ref) = rest[7:12]
    gmix_ref, tail_ref, edge_ref, dtaps_ref, now_ref, next_ref = rest[12:]
    gmix_ref[:RIM] = jnp.zeros((RIM, gmix_ref.shape[1]), LOW)
    mine = heads * HEAD
    chunks = seg_ref.shape[0]
    i_at, j_at = grid_index(0), grid_index(1)
    now_ref[...] = leave_ref[...]
    next_ref[...] = jnp.zeros_like(next_ref)
    dtaps_ref[...] = jnp.zeros_like(dtaps_ref)

    def one(step, carry):
        chunk = chunks - 1 - step
        start = pl.multiple_of(chunk * CHUNK, CHUNK)
        cols_far = cols_ref[pl.ds(start, CHUNK + SPAN), :]
        cols = cols_far[:CHUNK]
        same = cols[:, 4:5] == seg_ref[chunk]
        lower = (same & (j_at < i_at)).astype(FULL)
        inclusive = (same & (j_at <= i_at)).astype(FULL)
        carried, ending = cols[:, 5:6], cols[:, 6:7]
        last = mix_ref[here_rows(chunk), 4 * mine : 4 * mine + HEAD]
        dlast = jnp.zeros((CHUNK, HEAD), FULL)
        for head in range(heads):
            at = chunk * heads + head
            lows = [part * mine + head * HEAD for part in range(3)]
            mixed = [conv_part(mix_ref, taps_ref, cols, chunk, low) for low in lows]
            query, query_scale = unit_part(jax.nn.silu(mixed[0][0]))
            key, key_scale = unit_part(jax.nn.silu(mixed[1][0]))
            value = jax.nn.silu(mixed[2][0])
            weight = jax.nn.sigmoid(last[:, head : head + 1])
            leave = now_ref[head]
            now_ref[head] = mul(split(map_ref[at].T), split(leave)) + term_ref[at]
            ddelta = first_ref[at] + mul_once(key * ending, leave)
            solved = mul_once(inv_ref[at].T, ddelta)
            delta = delta_ref[at]
            dout = dout_ref[at]
            ends = jnp.concatenate([solved, dout], 0)
            by_state = mul_once_t(ends, p_ref[at])
            by_delta = mul_once_t(ends, delta)
            dright = -by_state[:CHUNK]
            dsystem = -by_delta[:CHUNK] * lower
            datt = by_delta[CHUNK:] * inclusive
            dquery = carried * by_state[CHUNK:] + mul_once(datt, key)
            gram = mul_once_t(key, key)
            dgram = weight * dsystem
            left = jnp.concatenate([datt.T, dgram + dgram.T], 1)
            right = jnp.concatenate([query, key], 0)
            dkey = mul_once(left, right) + (weight * carried) * dright
            dkey = dkey + ending * mul_once_t(delta, leave)
            dvalue = weight * solved
            dweight = row_sum(solved * value + carried * dright * key + dsystem * gram)
            dlogit = dweight * weight * (1.0 - weight)
            dlast = jnp.where(j_at == head, dlogit, dlast)
            dactive = [
                query_scale * (dquery - query * row_sum(dquery * query)),
                key_scale * (dkey - key * row_sum(dkey * key)),
                dvalue,
            ]
            for part, low in enumerate(lows):
                total, terms = mixed[part]
                dtotal = dactive[part] * silu_slope(total)
                here = slice(low, low + HEAD)
                far = jnp.concatenate([dtotal, next_ref[:, here]], 0)
                near = jnp.concatenate([jnp.zeros((SPAN, HEAD), FULL), dtotal[:SPAN]], 0)
                next_ref[:, here] = dtotal[:SPAN]
                dproj = jnp.zeros((CHUNK, HEAD), FULL)
                edge = jnp.zeros((SPAN, HEAD), FULL)
                zero = jnp.zeros((SPAN, 1), FULL)
                for tap in range(CONV):
                    back = CONV - 1 - tap
                    tap_row = taps_ref[tap : tap + 1, here]
                    dtaps_ref[tap : tap + 1, here] += jnp.sum(dtotal * terms[tap], axis=0, keepdims=True)
                    spread = far * cols_far[:, tap : tap + 1]
                    near_mask = jnp.concatenate([zero, cols[:SPAN, tap : tap + 1]], 0)
                    close = near * near_mask
                    if back > 0:
                        spread = pltpu.roll(spread, CHUNK + SPAN - back, 0)
                        close = pltpu.roll(close, 2 * SPAN - back, 0)
                        edge = edge + tap_row * close[:SPAN]
                    dproj = dproj + tap_row * spread[:CHUNK]
                gmix_ref[here_rows(chunk), here] = dproj.astype(LOW)
                edge_ref[:, here] = edge

                @pl.when(step == 0)
                def _():
                    tail_ref[:, here] = dproj[CHUNK - SPAN :]

        gmix_ref[here_rows(chunk), 3 * mine : 4 * mine] = dgate_ref[pl.ds(start, CHUNK), :]
        gmix_ref[here_rows(chunk), 4 * mine : 4 * mine + HEAD] = dlast.astype(LOW)
        return carry

    lax.fori_loop(0, chunks, one, 0)
    gap = jnp.zeros((RIM - SPAN, 3 * mine), FULL)
    gmix_ref[:RIM, : 3 * mine] = jnp.concatenate([gap, edge_ref[...]], 0).astype(LOW)


def on_chip(body, shapes, scratch, flops, waited, *operands):
    whole = pl.BlockSpec(memory_space=pltpu.VMEM)
    anywhere = pl.BlockSpec(memory_space=pl.ANY)
    used, spare = len(operands), len(waited)
    return pl.pallas_call(
        lambda *refs: body(*refs[:used], *refs[used + spare :]),
        out_shape=shapes,
        in_specs=[whole] * used + [anywhere] * spare,
        out_specs=[whole] * len(shapes),
        scratch_shapes=list(scratch),
        compiler_params=pltpu.CompilerParams(vmem_limit_bytes=56 * 1024 * 1024),
        cost_estimate=pl.CostEstimate(flops=flops, bytes_accessed=20 * 1024 * 1024, transcendentals=0),
    )(*operands, *waited)


def squares(*counts):
    return tuple(jax.ShapeDtypeStruct((count, HEAD, HEAD), FULL) for count in counts)


def delta_prep(heads, deep, mix, taps, cols, segs, waited):
    each = segs.shape[0] * heads
    shapes = squares(*[each] * 8, heads, heads)
    body = functools.partial(prep_kernel, heads, deep)
    return on_chip(body, shapes, (), 30 * MICRO, waited, mix, taps, cols, segs)


def delta_run(heads, mix, cols, gain, prepared, state, waited):
    q, k, uk, uv, inv, att, step, add = prepared
    each = q.shape[0]
    count = each // heads * CHUNK
    shapes = squares(each, each, each) + (jax.ShapeDtypeStruct((count, heads * HEAD), LOW),)
    body = functools.partial(run_kernel, heads)
    scratch = [pltpu.VMEM((heads, HEAD, HEAD), FULL)]
    flops = 11 * MICRO
    return on_chip(
        body, shapes, scratch, flops, waited, mix, cols, gain, q, uk, uv, att, step, add, state
    )


def delta_back(heads, mix, cols, gain, prepared, output, grad, waited):
    q, k, uk, uv, inv, att, step, add = prepared
    each = q.shape[0]
    count = each // heads * CHUNK
    mine = heads * HEAD
    shapes = squares(each, each, each) + (
        jax.ShapeDtypeStruct((count, mine), LOW),
    ) + squares(heads)
    body = functools.partial(back_kernel, heads)
    flops = 12 * MICRO
    return on_chip(
        body, shapes, (), flops, waited, mix, cols, gain, q, uk, att, step, output, grad
    )


def delta_pull(heads, mix, taps, cols, segs, prepared, states, delta, backs, leaving, waited):
    q, k, uk, uv, inv, att, step, add = prepared
    dout, first, term, dgate = backs
    mine = heads * HEAD
    shapes = (
        jax.ShapeDtypeStruct(mix.shape, LOW),
        jax.ShapeDtypeStruct((SPAN, 3 * mine), FULL),
        jax.ShapeDtypeStruct((SPAN, 3 * mine), FULL),
        jax.ShapeDtypeStruct((SPAN, 3 * mine), FULL),
    )
    body = functools.partial(pull_kernel, heads)
    scratch = [pltpu.VMEM((heads, HEAD, HEAD), FULL), pltpu.VMEM((SPAN, 3 * mine), FULL)]
    flops = 30 * MICRO
    return on_chip(
        body, shapes, scratch, flops, waited, mix, taps, cols, segs, q, k, inv, att, step, states, delta, dout, first, term, dgate, leaving
    )


def swiglu(gate_two, up_two):
    return jax.nn.silu(gate_two) * up_two


def local(
    block_input,
    segments,
    mix_gain,
    w_project,
    conv_taps,
    w_beta,
    w_gate,
    head_gain,
    w_output,
    ffn_gain,
    w_hidden_gate,
    w_hidden_up,
    w_hidden_down,
    cotangent,
):
    dp, seq = lax.axis_size("dp"), lax.axis_size("seq")
    width = min(WIDTH, seq & -seq)
    cubes = seq // width
    everyone = dp * seq
    fiber = dp * cubes
    both = ("dp", "seq")
    row_at, chip_at = lax.axis_index("dp"), lax.axis_index("seq")
    me = chip_at % width
    cube_at = chip_at // width
    heads = H // width
    mine = heads * HEAD
    rows = w_project.shape[0]
    tokens = block_input.shape[1]
    count = tokens * width
    units = w_hidden_down.shape[0]
    hidden_mine = fiber * units

    taps_each = conv_taps.shape[1]
    packed = jnp.concatenate(
        [
            mix_gain.astype(LOW),
            head_gain.astype(LOW),
            ffn_gain.astype(LOW),
            conv_taps.astype(LOW).reshape(-1),
            segments[0].astype(LOW),
        ]
    )
    mixer_pad = -(mine * 4 + heads) % 128
    mixer_low = jnp.concatenate(
        [
            jnp.swapaxes(w_project.reshape(rows, 3, width, mine), 1, 2).reshape(rows, width, 3 * mine),
            w_gate.reshape(rows, width, mine),
            w_beta.reshape(rows, width, heads),
            jnp.zeros((rows, width, mixer_pad), FULL),
        ],
        -1,
    ).astype(LOW)
    mixer_turned = cube_turn(jnp.swapaxes(mixer_low, 0, 1), width)
    small = gather_all(packed)
    gain_one = small[:, :rows].reshape(D).astype(FULL)
    gain_head = small[:, rows : 2 * rows].reshape(D).astype(FULL)
    gain_two = small[:, 2 * rows : 3 * rows].reshape(D).astype(FULL)
    taps_full = small[:, 3 * rows : 3 * rows + CONV * taps_each].reshape(everyone, CONV, taps_each)
    taps_full = jnp.swapaxes(taps_full, 0, 1).reshape(CONV, 3, width, mine).astype(FULL)
    taps_mine = lax.dynamic_index_in_dim(taps_full, me, 2, False).reshape(CONV, 3 * mine)
    gain_mine = lax.dynamic_index_in_dim(gain_head.reshape(width, heads, HEAD), me, 0, False)
    seg_all = small[:, 3 * rows + CONV * taps_each :].astype(jnp.int32).reshape(dp, seq * tokens)
    seg_row = lax.dynamic_index_in_dim(seg_all, row_at, 0, False)
    ext_seg = lax.dynamic_slice_in_dim(
        jnp.concatenate([jnp.zeros((CONV - 1,), jnp.int32), seg_row]),
        cube_at * count,
        count + CONV - 1,
    )
    seg_mine = ext_seg[CONV - 1 :]
    tokens_in = jnp.concatenate([fiber_order(block_input, width), cotangent], 0)
    pair = cube_gather(tokens_in, width, 2)
    x_cube, g_out = pair[0], pair[1]
    ahead = [(i, i + width) for i in range(seq - width)]
    behind = [(i + width, i) for i in range(seq - width)]
    rim = lax.ppermute(fiber_order(x_cube[count - RIM :], width), "seq", ahead)
    x_more = jnp.concatenate([fiber_order(rim, width), x_cube], 0)
    mixer_far = near_gather(mixer_turned, "seq", width, cubes)
    mixer_w = near_gather(mixer_far, "dp", 1, dp).reshape(D, -1)

    hgate_late, hup_late = hint((w_hidden_gate, w_hidden_up), mixer_turned)

    def by_units(weight):
        split = weight.astype(LOW).reshape(rows, dp, cubes, width, units)
        return jnp.transpose(split, (3, 0, 1, 2, 4)).reshape(width, rows, hidden_mine)

    ffn_low = jnp.concatenate([by_units(hgate_late), by_units(hup_late)], -1)
    ffn_turned = cube_turn(ffn_low, width)
    ffn_far = near_gather(hint(ffn_turned, mixer_far), "seq", width, cubes)

    residual = block_input[0].astype(FULL)
    normed_own, mix_pull = jax.vjp(lambda v: rms_scale(v, gain_one), residual)
    normed = rms_scale(x_more.astype(FULL), fiber_order(gain_one, width)).astype(LOW)
    mixed_in = dot_low(normed, mixer_w)
    out_low, down_low, mixed_in = lax.optimization_barrier(
        (w_output.astype(LOW), w_hidden_down.astype(LOW), mixed_in)
    )
    out_far = near_gather(out_low, "seq", width, cubes)
    out_spread = jnp.broadcast_to(out_far[None], (width,) + out_far.shape)
    out_near = cube_turn(out_spread, width).reshape(D // dp, D)
    chunks = count // CHUNK
    seg_chunks = seg_mine.reshape(chunks, CHUNK)
    before = jnp.concatenate([ext_seg[CONV - 2 : CONV - 1], seg_chunks[:-1, -1]], 0)
    columns = [ext_seg[tap : tap + count] == seg_mine for tap in range(CONV)]
    columns.append(seg_mine)
    columns.append((seg_chunks == before[:, None]).reshape(count))
    columns.append((seg_chunks == seg_chunks[:, -1:]).reshape(count))
    columns.append(jnp.zeros((count,), FULL))
    cols = jnp.stack([column.astype(FULL) for column in columns], 1)
    cols = jnp.pad(cols, ((0, SPAN), (0, 0)))
    segs = seg_chunks.astype(FULL)[:, None, :]
    gain_row = gain_mine.reshape(1, mine)
    prepared = delta_prep(heads, cubes > 2, mixed_in, taps_mine, cols, segs, ())
    far, end = prepared[8:]
    prepared = prepared[:8]
    state_in = jnp.zeros((heads, HEAD, HEAD), FULL)
    for hop in range(cubes - 1):
        out = end
        if hop > 0:
            out = end + jnp.einsum("hij,hjk->hik", far, state_in, precision=HIGH)
        state_in = lax.ppermute(out, "seq", ahead)
    states, delta, recalled, scaled = delta_run(
        heads, mixed_in, cols, gain_row, prepared, state_in, ()
    )
    ffn_w = near_gather(ffn_far, "dp", 1, dp).reshape(D, 2 * hidden_mine)
    out_parts = [out_near]
    for bit in bits_of(dp):
        out_parts = out_parts + [swap(part, "dp", bit) for part in out_parts]
    scaled_own = jnp.swapaxes(cube_turn(scaled.reshape(width, tokens, mine), width), 0, 1)
    down_w = chip_gather(fiber_gather_seq(down_low, width)).reshape(hidden_mine, D)
    scaled_own = fiber_order(scaled_own.reshape(tokens, D), width)
    scaled_own = jnp.swapaxes(scaled_own.reshape(tokens, dp, cubes, width, rows), 2, 3)
    scaled_own = scaled_own.reshape(tokens, dp, D // dp)
    middle = residual
    for at, part in enumerate(out_parts):
        middle = middle + dot_low(scaled_own[:, at], part)

    normed_two_f, ffn_pull = jax.vjp(lambda v: rms_scale(v, gain_two), middle)
    normed_two = cube_gather(fiber_order(normed_two_f.astype(LOW), width), width, 3)
    both_two = dot_low(normed_two, ffn_w)
    gate_two, up_two = both_two[:, :hidden_mine], both_two[:, hidden_mine:]
    hidden_f, glu_pull = jax.vjp(swiglu, gate_two, up_two)
    hidden = hidden_f.astype(LOW)
    grad_hidden = dot_right_t(g_out, down_w)
    grad_gate_two, grad_up_two = glu_pull(grad_hidden)
    grad_both = jnp.concatenate([grad_gate_two.astype(LOW), grad_up_two.astype(LOW)], 1)
    pulled = dot_right_t(grad_both, ffn_w).astype(LOW)
    grad_normed_two = fiber_order(cube_sum(pulled, width), width)
    grad_down = chip_sum(dot_left_t(hidden, g_out).reshape(fiber, units, D))
    grad_ffn = dot_left_t(normed_two, grad_both).reshape(dp, cubes, width, rows, -1)
    grad_ffn = near_sum(grad_ffn, "dp", 1, dp)
    grad_normed_two, grad_ffn, grad_down = lax.optimization_barrier(
        (grad_normed_two, grad_ffn, grad_down)
    )
    (grad_middle,) = ffn_pull(grad_normed_two)
    grad_middle = grad_middle + cotangent[0].astype(FULL)
    grad_branch = grad_middle.astype(LOW)
    grad_scaled_own = jnp.stack([dot_right_t(grad_branch, part).astype(LOW) for part in out_parts], 1)
    grad_scaled_own = jnp.swapaxes(grad_scaled_own.reshape(tokens, dp, width, cubes, rows), 2, 3)
    grad_scaled_own = fiber_order(grad_scaled_own.reshape(tokens, D), width)

    grad_scaled = cube_turn(
        jnp.swapaxes(grad_scaled_own.reshape(tokens, width, mine), 0, 1), width
    ).reshape(count, mine)
    owners = []
    for row in range(dp):
        for chip in range(seq):
            block = (chip % width) * fiber + row * cubes + chip // width
            owners.append((row * seq + chip, block))
    groups = [list(range(first, first + width)) for first in range(0, seq, width)]
    branch_cube = cube_turn(jnp.broadcast_to(tie(grad_branch, grad_scaled)[None], (width, tokens, D)), width)
    branch_cube = branch_cube.reshape(count, D)
    half = D // len(cube_orders(width, 2))
    down_parts = [down_w[:, at : at + half] for at in range(0, D, half)]
    backs = delta_back(
        heads, mixed_in, cols, gain_row, prepared, recalled, grad_scaled, ()
    )
    end_back = backs[4]
    leaving = jnp.zeros((heads, HEAD, HEAD), FULL)
    for hop in range(cubes - 1):
        out = end_back
        if hop > 0:
            out = end_back + jnp.einsum("hji,hjk->hik", far, leaving, precision=HIGH)
        leaving = lax.ppermute(out, "seq", behind)
    grad_ffn = near_sum(grad_ffn, "seq", width, cubes, (leaving,)).astype(LOW)
    grad_mixed, tail, edge, grad_taps = delta_pull(
        heads, mixed_in, taps_mine, cols, segs, prepared, states, delta, backs[:4], leaving,
        (),
    )
    result = middle + cube_sum_by_axes(tie(hidden, edge), down_parts, dot_low, width)
    block_output = result.astype(LOW)[None]
    grad_mixed = tie(grad_mixed, branch_cube)
    grad_mixer = dot_left_t(normed, grad_mixed).reshape(dp, cubes, width, rows, -1)
    grad_mixer = near_sum(grad_mixer, "dp", 1, dp)
    from_next = lax.ppermute(edge.astype(LOW), "seq", behind).astype(FULL)
    grad_fixed = lax.dynamic_update_slice(
        grad_mixed[RIM:], (tail + from_next).astype(LOW), (count - SPAN, 0)
    )
    grad_taps = grad_taps[:CONV]
    grad_fixed = tie(grad_fixed, grad_mixer)
    mixer_parts = [mixer_w[at : at + half] for at in range(0, D, half)]
    grad_oproj = chip_sum(dot_left_t(scaled, branch_cube).reshape(fiber, rows, D))
    grad_oproj = far_sum(grad_oproj, width, (grad_ffn,))
    grad_mixer = near_sum(grad_mixer, "seq", width, cubes, (grad_ffn, grad_oproj)).astype(LOW)
    mixer_far_sum = grad_mixer
    grad_normed = cube_sum_by_axes(grad_fixed, mixer_parts, dot_right_t, width)
    grad_normed = fiber_order(grad_normed, width)
    grad_oproj = lax.ppermute(grad_oproj.astype(LOW), both, owners).astype(FULL)
    grad_ffn = cube_turn(tie(grad_ffn, grad_normed), width)
    taps_wide = lax.dynamic_update_index_in_dim(
        jnp.zeros((CONV, 3, width, mine), FULL), grad_taps.reshape(CONV, 3, mine), me, 2
    ).reshape(CONV, everyone, taps_each)
    taps_wide = jnp.swapaxes(taps_wide, 0, 1).reshape(everyone, CONV * taps_each)
    taps_own = sum_all(taps_wide)
    grad_mixer = cube_turn(tie(grad_mixer, grad_ffn, taps_own, block_output), width).astype(FULL)
    grad_ffn = grad_ffn.astype(FULL)

    def by_rows(grad):
        split = grad.reshape(width, rows, dp, cubes, units)
        return jnp.transpose(split, (1, 2, 3, 0, 4)).reshape(rows, -1)

    grad_hgate, grad_hup = by_rows(grad_ffn[..., :hidden_mine]), by_rows(grad_ffn[..., hidden_mine:])
    grad_mixer = jnp.swapaxes(grad_mixer, 0, 1)
    grad_wproj = jnp.swapaxes(grad_mixer[..., : 3 * mine].reshape(rows, width, 3, mine), 1, 2)
    grad_wproj = grad_wproj.reshape(rows, 3 * D)
    grad_wgate = grad_mixer[..., 3 * mine : 4 * mine].reshape(rows, D)
    grad_wbeta = grad_mixer[..., 4 * mine : 4 * mine + heads].reshape(rows, H)
    grad_down = far_sum(grad_down, width, (mixer_far_sum,), (grad_hgate, grad_hup))
    (grad_tokens,) = mix_pull(grad_normed)
    grad_input = (grad_tokens + grad_middle)[None]

    def gain_grad(gain, *pairs):
        terms = [row_sum(weight.astype(LOW).astype(FULL) * grad) for weight, grad in pairs]
        return sum(terms)[:, 0] / gain.astype(LOW).astype(FULL)

    grad_mgain = gain_grad(mix_gain, (w_project, grad_wproj), (w_gate, grad_wgate), (w_beta, grad_wbeta))
    grad_hgain = gain_grad(head_gain, (w_output, grad_oproj))
    grad_fgain = gain_grad(ffn_gain, (w_hidden_gate, grad_hgate), (w_hidden_up, grad_hup))
    return (
        block_output,
        grad_input,
        grad_mgain,
        grad_wproj,
        taps_own.reshape(CONV, taps_each),
        grad_wbeta,
        grad_wgate,
        grad_hgain,
        grad_oproj,
        grad_fgain,
        grad_hgate,
        grad_hup,
        grad_down,
    )


def solution(mesh):
    tokens = P("dp", "seq", None)
    vector = P(("dp", "seq"))
    matrix = P(("dp", "seq"), None)
    taps = P(None, ("dp", "seq"))
    in_specs = (tokens, P("dp", "seq"), vector, matrix, taps, matrix, matrix, vector, matrix)
    in_specs = in_specs + (vector, matrix, matrix, matrix, tokens)
    out_specs = (tokens, tokens, vector, matrix, taps, matrix, matrix, vector, matrix)
    out_specs = out_specs + (vector, matrix, matrix, matrix)
    return jax.shard_map(local, mesh=mesh, in_specs=in_specs, out_specs=out_specs, check_vma=False)
```
